128 devices in a mesh: user: 8 (over z_hi, x), cand: 8 (over z_lo, y), tensor: 2 (over core).
Axes of the slice: x: 4, y: 4, z: 4 (z_hi: 2, z_lo: 2; z = z_hi * 2 + z_lo), core: 2. Of those that a mesh axis runs over, the one named last changes fastest.
Arguments:
- cand_embed: bfloat16 [8, 4096, 1024], P('user', 'cand'), may hold values from -6 to 6
- cand_ids: int32 [8, 4096], P('user', 'cand'), may hold values from 0 to 255
- hist_ids: int32 [8, 4096], P('user', ('cand', 'tensor')), may hold values from 0 to 255
- hist_len: int32 [8], P('user'), may hold values from 1 to 4096, as said below
- hist_keys: bfloat16 [8, 2, 4096, 1024], P('user', None, ('cand', 'tensor')), may hold values from -6 to 6
- hist_values: bfloat16 [8, 2, 4096, 1024], P('user', None, ('cand', 'tensor')), may hold values from -6 to 6
- w_in: bfloat16 [2, 1024, 4, 1024], P(None, None, None, 'tensor'), may hold values from -0.1875 to 0.1875
- w_out: bfloat16 [2, 1024, 1024], P(None, 'tensor'), may hold values from -0.1875 to 0.1875
Outputs:
- cand_out: float32 [8, 4096, 1024], P('user', 'cand')
The draws below stay inside these ranges and needn't reach their ends.
Inputs may be any that keep to these rules, and one draw needn't show every extreme that they name: `hist_len`: some user has exactly 4096 live history positions.
All inputs are finite; a program needn't handle non-finite values.
Results may differ from the reference program's by a relative error of at most 0.017.
Values may be sent and summed in bfloat16 or wider, within the bound.
A program may use at most 128 MiB of HBM per device.

```python
import math
import jax
import jax.numpy as jnp
import numpy as np
from jax import lax

D = 1024
HEADS = 8
LAYERS = 2
HIST = 4096
ITEM_RANGE = 256
USERS = 8
CANDS = 4096
N_TENSOR = 2


def draw_hist_len(key, part):
    key = jax.random.fold_in(key, 11)
    first, second = jax.random.split(key)
    lengths = jax.random.randint(first, (USERS,), 1, HIST + 1, dtype=jnp.int32)
    chosen = jax.random.randint(second, (), 0, USERS, dtype=jnp.int32)
    return jnp.where(jnp.arange(USERS, dtype=jnp.int32) == chosen, HIST, lengths).astype(jnp.int32)


def touch_ends(array, stream_key, least, top_value):
    index_at = [jax.random.randint(jax.random.fold_in(stream_key, axis), (), 0, length) for axis, length in enumerate(array.shape)]
    widest = array.shape.index(max(array.shape))
    next_to = index_at[:widest] + [(index_at[widest] + 1) % array.shape[widest]] + index_at[widest + 1:]
    return array.at[tuple(index_at)].set(least).at[tuple(next_to)].set(top_value)


def shard_levels(stream_key, shape, cuts, low, top_value):
    def one(axis_at, shards_of):
        steps = jax.random.uniform(jax.random.fold_in(jax.random.fold_in(stream_key, 6), axis_at), (shards_of,), jnp.float32, low / len(cuts), top_value / len(cuts))
        return jnp.repeat(jnp.exp(steps), shape[axis_at] // shards_of).reshape((-1,) + (1,) * (len(shape) - axis_at - 1))

    gain = one(*cuts[0])
    for cut in cuts[1:]:
        gain = gain * one(*cut)
    return gain


def rank_table(count, lean):
    weights = [(1 << 20) // math.isqrt(grade ** lean) + 1 for grade in range(1, count + 1)]
    width = 1 + sum(weights) // (1 << 30)
    return np.cumsum(np.array([max(1, weight // width) for weight in weights]))


def skewed_ids(key, extent, number_of, skew):
    grid = rank_table(number_of, skew)
    lot = jax.random.randint(jax.random.fold_in(key, 1), extent, 0, int(grid[number_of - 1]))
    grade = jnp.searchsorted(jnp.asarray(grid, jnp.int32), lot, side="right")
    return jax.random.permutation(jax.random.fold_in(key, 2), number_of)[grade].astype(jnp.int32)


def normal_values(rng, dims, deviation, bound, shards=(), held_as=jnp.bfloat16):
    array = jax.random.normal(rng, dims, jnp.float32) * deviation
    if len(shards) > 0:
        array = shard_levels(rng, dims, shards, -0.22, 0.18) * array
    return jnp.clip(array, min=-bound, max=bound).astype(held_as)


def setup_inputs(seed: int = 0) -> dict:
    seeds = jax.random.split(jax.random.key(seed), 9)
    cand_embed = normal_values(seeds[0], (USERS, CANDS, D), 1.0, 6.0, ((0, 8), (1, 8)))
    cand_ids = touch_ends(skewed_ids(seeds[1], (USERS, CANDS), ITEM_RANGE, 4), jax.random.fold_in(seeds[1], 3), 0, ITEM_RANGE - 1).astype(jnp.int32)
    hist_ids = touch_ends(skewed_ids(seeds[2], (USERS, HIST), ITEM_RANGE, 4), jax.random.fold_in(seeds[2], 3), 0, ITEM_RANGE - 1).astype(jnp.int32)
    hist_len = draw_hist_len(jax.random.fold_in(seeds[8], 71), 0)
    hist_keys = normal_values(seeds[4], (USERS, LAYERS, HIST, D), 1.0, 6.0, ((0, 8), (2, 16)))
    hist_values = normal_values(seeds[5], (USERS, LAYERS, HIST, D), 1.0, 6.0, ((0, 8), (2, 16)))
    w_in = normal_values(seeds[6], (LAYERS, D, 4, D), D ** -0.5, 0.1875, ((3, 2),))
    w_out = normal_values(seeds[7], (LAYERS, D, D), D ** -0.5, 0.1875, ((1, 2),))
    return dict(cand_embed=cand_embed, cand_ids=cand_ids, hist_ids=hist_ids, hist_len=hist_len, hist_keys=hist_keys, hist_values=hist_values, w_in=w_in, w_out=w_out)


def row_norm(values):
    return values * lax.rsqrt(lax.optimization_barrier(jnp.mean(values * values, axis=-1, keepdims=True)) + 1e-06)

def layer_user(state, keys, values, hist_item, length, cand_item, weight_in, weight_out):
    count = state.shape[0]
    head_dim = D // HEADS
    scale = head_dim ** (-0.5)
    normed = row_norm(state).astype(jnp.bfloat16)
    proj = jax.nn.silu(jnp.dot(normed, weight_in.reshape(D, 4 * D), preferred_element_type=jnp.float32))
    proj = proj.reshape(count, 4, D)
    gate_u = proj[:, 0]
    value_b = proj[:, 1].astype(jnp.bfloat16)
    query_b = proj[:, 2].astype(jnp.bfloat16)
    key_b = proj[:, 3].astype(jnp.bfloat16)
    query_h = query_b.reshape(count, HEADS, head_dim).transpose(1, 0, 2)
    key_h = keys.reshape(HIST, HEADS, head_dim).transpose(1, 0, 2)
    value_h = values.reshape(HIST, HEADS, head_dim).transpose(1, 0, 2)
    positions = jnp.arange(HIST, dtype=jnp.int32)
    valid = (positions < length)[None, :] & (hist_item[None, :] != cand_item[:, None])

    def one_head(items):
        query_one, key_one, value_one = items
        scores = jnp.einsum('cd,pd->cp', query_one, key_one, preferred_element_type=jnp.float32) * scale
        weights = jnp.where(valid, jax.nn.silu(scores), 0.0).astype(jnp.bfloat16)
        return jnp.dot(weights, value_one, preferred_element_type=jnp.float32)
    hist_part = lax.map(one_head, (query_h, key_h, value_h)).transpose(1, 0, 2)
    own_scores = lax.optimization_barrier(jnp.sum(query_b.astype(jnp.float32).reshape(count, HEADS, head_dim) * key_b.astype(jnp.float32).reshape(count, HEADS, head_dim), axis=-1)) * scale
    own_part = jax.nn.silu(own_scores)[..., None] * value_b.astype(jnp.float32).reshape(count, HEADS, head_dim)
    attended = (hist_part + own_part).reshape(count, D)
    normed_z = row_norm(attended * gate_u).astype(jnp.bfloat16)
    block = D // N_TENSOR
    total = jnp.zeros((count, D), jnp.float32)
    for part_index in range(N_TENSOR):
        piece = jnp.dot(normed_z[:, part_index * block:(part_index + 1) * block], weight_out[part_index * block:(part_index + 1) * block], preferred_element_type=jnp.float32)
        total = total + lax.optimization_barrier(piece.astype(jnp.bfloat16)).astype(jnp.float32)
    return state + total

def reference(cand_embed, cand_ids, hist_ids, hist_len, hist_keys, hist_values, w_in, w_out):

    def one_user(items):
        embed, cand_item, hist_item, length, keys, values = items
        state = embed.astype(jnp.float32)
        for layer in range(LAYERS):
            state = layer_user(state, keys[layer], values[layer], hist_item, length, cand_item, w_in[layer], w_out[layer])
        return state
    return lax.map(one_user, (cand_embed, cand_ids, hist_ids, hist_len, hist_keys, hist_values))
```

```python
import functools

import jax
import jax.numpy as jnp
from jax import lax
from jax.experimental import pallas as pl
from jax.experimental.pallas import tpu as pltpu
from jax.sharding import PartitionSpec as P

HEADS = 8
LAYERS = 2
BF = jnp.bfloat16
F32 = jnp.float32
SELF, LEFT, RIGHT, FAR = 0, 1, 2, 3


def gated(half):
    return half + half * jnp.tanh(half)


def kernel(
    dims,
    len_ref,
    embed_hbm,
    cid_hbm,
    hid_hbm,
    key_hbm,
    val_hbm,
    win_hbm,
    wout_hbm,
    out_hbm,
    kv,
    qown,
    qrem,
    psend,
    precv,
    zbuf,
    kown,
    vown,
    uown,
    win,
    wout,
    embed,
    state,
    normed,
    mask,
    cids,
    hids,
    acc,
    kv_recv,
    kv_send,
    q_recv,
    q_send,
    p_recv,
    p_send,
    z_recv,
    z_send,
    w_sem,
    wo_sem,
    wo_recv,
    id_recv,
    id_send,
    loc_sem,
    out_sem,
):
    ring, rows, here, width, head = dims
    local = here * head
    count = state.shape[0]
    units = LAYERS * here
    scale = head ** (-0.5)

    cand = lax.axis_index("cand")
    t = lax.axis_index("tensor")
    y = lax.rem(cand, ring)
    plane = cand - y
    right = plane + lax.rem(y + 1, ring)
    left = plane + lax.rem(y + ring - 1, ring)
    far = plane + lax.rem(y + 2, ring)
    across = lax.rem(cand + ring, 2 * ring)

    peers = [(cand, 1 - t), (across, t)]
    for chip in (left, right, far):
        peers += [(chip, 0), (chip, 1)]

    embed_copy = pltpu.make_async_copy(embed_hbm, embed, loc_sem.at[0])
    embed_copy.start()

    def win_copy(layer, j):
        return pltpu.make_async_copy(win_hbm.at[layer, j], win.at[layer, j], w_sem.at[layer, j])

    win_copy(0, 2).start()

    barrier = pltpu.get_barrier_semaphore()
    for chip, core in peers:
        pl.semaphore_signal(barrier, inc=1, device_id={"cand": chip, "tensor": core})
    pl.semaphore_wait(barrier, len(peers))

    def remote(src, dst, send, recv, chip, core):
        return pltpu.make_async_remote_copy(
            src_ref=src,
            dst_ref=dst,
            send_sem=send,
            recv_sem=recv,
            device_id={"cand": chip, "tensor": core},
        )

    def wait(ref, sem):
        pltpu.make_async_copy(ref, ref, sem).wait()

    hid_local = pltpu.make_async_copy(hid_hbm, hids.at[SELF * 2 + t], loc_sem.at[1])
    cid_local = pltpu.make_async_copy(cid_hbm, cids.at[1], loc_sem.at[2])
    hid_local.start()
    cid_local.start()
    id_copies = [remote(cid_hbm, cids.at[0], id_send.at[0], id_recv.at[8], across, t)]
    targets = [
        (cand, 1 - t, SELF),
        (right, 0, LEFT),
        (right, 1, LEFT),
        (left, 0, RIGHT),
        (left, 1, RIGHT),
        (far, 0, FAR),
        (far, 1, FAR),
    ]
    for i, (chip, core, origin) in enumerate(targets):
        slot = origin * 2 + t
        id_copies.append(
            remote(hid_hbm, hids.at[slot], id_send.at[1 + i], id_recv.at[slot], chip, core)
        )
    for copy in id_copies:
        copy.start()

    def direct(u):
        layer, h = u // here, lax.rem(u, here)
        own = pl.ds(pl.multiple_of(t * local + h * head, head), head)
        other = pl.ds(pl.multiple_of((1 - t) * local + h * head, head), head)
        mine = SELF * 2 + t
        for i, src in enumerate((key_hbm, val_hbm)):
            for chip, origin in ((right, LEFT), (left, RIGHT)):
                slot = origin * 2 + t
                for core in (0, 1):
                    cols = pl.ds(core * local + pl.multiple_of(h * head, head), head)
                    remote(
                        src.at[layer, :, cols],
                        kv.at[u, slot, i],
                        kv_send.at[u, 0],
                        kv_recv.at[u, slot],
                        chip,
                        core,
                    ).start()
            remote(
                src.at[layer, :, other],
                kv.at[u, mine, i],
                kv_send.at[u, 1],
                kv_recv.at[u, mine],
                cand,
                1 - t,
            ).start()
            pltpu.make_async_copy(
                src.at[layer, :, own], kv.at[u, mine, i], kv_recv.at[u, mine]
            ).start()

    def forward(u):
        wait(kv.at[u, 2], kv_recv.at[u, 2])
        remote(kv.at[u, 2], kv.at[u, 6], kv_send.at[u, 2], kv_recv.at[u, 6], right, t).start()
        wait(kv.at[u, 5], kv_recv.at[u, 5])
        remote(kv.at[u, 5], kv.at[u, 7], kv_send.at[u, 3], kv_recv.at[u, 7], left, t).start()

    direct(0)
    direct(1)

    for j in (3, 1, 0):
        win_copy(0, j).start()

    own_half = pl.ds(pl.multiple_of(t * local, local), local)

    def wout_copies(layer):
        src, dst = wout_hbm.at[layer], wout.at[layer, own_half]
        return (
            pltpu.make_async_copy(src, dst, wo_sem.at[layer]),
            remote(src, dst, wo_sem.at[2 + layer], wo_recv.at[layer], cand, 1 - t),
        )

    BLOCK = 128

    def row_blocks(body):
        def step(i, _):
            body(pl.ds(pl.multiple_of(i * BLOCK, BLOCK), BLOCK))
            return 0

        lax.fori_loop(0, count // BLOCK, step, 0)

    def normalise(x):
        return (x * lax.rsqrt(jnp.mean(x * x, axis=-1, keepdims=True) + 1e-06)).astype(BF)

    embed_copy.wait()

    def first(block):
        x = embed[block, :].astype(F32)
        state[block, :] = x
        normed[block, :] = normalise(x)

    row_blocks(first)

    def project(layer, j, store):
        win_copy(layer, j).wait()

        def body(block):
            s = jnp.dot(normed[block, :], win[layer, j], preferred_element_type=F32)
            store(block, gated(0.5 * s))

        row_blocks(body)

    def queries(layer):
        def store(block, value):
            value = (value * (0.5 * scale)).astype(BF)
            for h in range(here):
                qown[layer, h, block, :] = value[:, h * head : (h + 1) * head]

        project(layer, 2, store)
        for h in range(here):
            remote(
                qown.at[layer, h],
                qrem.at[layer, h],
                q_send.at[layer, h],
                q_recv.at[layer, h],
                across,
                t,
            ).start()

    def others(layer):
        for j, ref in ((3, kown), (1, vown), (0, uown)):

            def store(block, value, ref=ref):
                value = value.astype(ref.dtype)
                for h in range(here):
                    ref[h, block, :] = value[:, h * head : (h + 1) * head]

            project(layer, j, store)

    queries(0)
    forward(0)
    direct(2)
    others(0)

    for copies in (wout_copies(0), wout_copies(1)):
        for copy in copies:
            copy.start()
    for j in (2, 3, 1, 0):
        win_copy(1, j).start()

    hid_local.wait()
    cid_local.wait()
    wait(cids.at[0], id_recv.at[8])
    wait(hids.at[SELF * 2 + 1 - t], id_recv.at[SELF * 2 + 1 - t])
    for slot in range(2, 8):
        wait(hids.at[slot], id_recv.at[slot])
    length = len_ref[0]
    for side in range(2):
        column = jnp.broadcast_to(cids[side].astype(F32), (128, count)).T

        def one_slot(slot, _, side=side, column=column):
            origin = slot // 2
            shift = jnp.where(origin == LEFT, ring - 1, jnp.where(origin == FAR, 2, 0))
            shift = jnp.where(origin == RIGHT, 1, shift)
            start = ((plane + lax.rem(y + shift, ring)) * 2 + lax.rem(slot, 2)) * rows
            for part in range(rows // 128):
                piece = slice(part * 128, (part + 1) * 128)
                ids = hids[slot, :, piece].astype(F32)
                at = start + part * 128 + lax.broadcasted_iota(jnp.int32, (1, 128), 1)
                live = jnp.where(at < length, 1.0, 0.0).astype(F32)
                mask[side, slot, :, piece] = jnp.where(column == ids, 0.0, live).astype(BF)
            return 0

        lax.fori_loop(0, 8, one_slot, 0)

    def attend(side, layer, h, u, low, high):
        q = (qrem, qown)[side].at[layer, h]

        def body(slot, _):
            half = lax.dot_general(
                q[...], kv[u, slot, 0], (((1,), (1,)), ((), ())), preferred_element_type=F32
            )
            weights = gated(half).astype(BF) * mask[side, slot]
            acc[side] += jnp.dot(weights, kv[u, slot, 1], preferred_element_type=F32)
            return 0

        lax.fori_loop(low, high, body, 0)

    def finish_head(layer, h):
        wait(precv.at[layer, h], p_recv.at[layer, h])

    for layer in range(LAYERS):

        def one_head(h, _, layer=layer):
            u = layer * here + h
            if layer == 0:
                forward(u + 1)
                direct(u + 3)
            else:

                @pl.when(h < 2)
                def _():
                    forward(u + 2)

            wait(kv.at[u, 0], kv_recv.at[u, 0])
            wait(kv.at[u, 1], kv_recv.at[u, 1])
            wait(kv.at[u, 3], kv_recv.at[u, 3])
            wait(kv.at[u, 4], kv_recv.at[u, 4])
            wait(qrem.at[layer, h], q_recv.at[layer, h])
            acc[...] = jnp.zeros_like(acc)
            attend(0, layer, h, u, 0, 6)
            attend(1, layer, h, u, 0, 6)
            wait(kv.at[u, 6], kv_recv.at[u, 6])
            wait(kv.at[u, 7], kv_recv.at[u, 7])
            attend(0, layer, h, u, 6, 8)
            psend[layer, h] = acc[0].astype(BF)
            remote(
                psend.at[layer, h],
                precv.at[layer, h],
                p_send.at[layer, h],
                p_recv.at[layer, h],
                across,
                t,
            ).start()
            attend(1, layer, h, u, 6, 8)
            q = qown[layer, h].astype(F32)
            own = gated(jnp.sum(q * kown[h].astype(F32), axis=-1, keepdims=True))
            part = acc[1] + own * vown[h].astype(F32)
            wait(precv.at[layer, h], p_recv.at[layer, h])
            gate = uown[h].astype(F32)
            cols = pl.ds(pl.multiple_of(t * local + h * head, head), head)
            zbuf[layer, :, cols] = ((part + precv[layer, h].astype(F32)) * gate).astype(BF)
            remote(
                zbuf.at[layer, :, cols],
                zbuf.at[layer, :, cols],
                z_send.at[layer, h],
                z_recv.at[layer, h],
                cand,
                1 - t,
            ).start()
            return 0

        lax.fori_loop(0, here, one_head, 0)

        if layer == 0:
            forward(here + 1)
            direct(here + 3)

        for copy in wout_copies(layer)[:1]:
            copy.wait()
        other_half = pl.ds(pl.multiple_of((1 - t) * local, local), local)
        wait(wout.at[layer, other_half], wo_recv.at[layer])
        for h in range(here):
            cols = pl.ds(pl.multiple_of((1 - t) * local, local) + h * head, head)
            wait(zbuf.at[layer, :, cols], z_recv.at[layer, h])

        def last(block, layer=layer):
            z = zbuf[layer, block, :]
            zf = z.astype(F32)
            size = lax.rsqrt(jnp.mean(zf * zf, axis=-1, keepdims=True) + 1e-06)
            x = state[block, :] + size * jnp.dot(z, wout[layer], preferred_element_type=F32)
            state[block, :] = x
            if layer + 1 < LAYERS:
                normed[block, :] = normalise(x)
            else:
                pltpu.make_async_copy(state.at[block], out_hbm.at[block], out_sem).start()

        row_blocks(last)
        if layer + 1 < LAYERS:
            queries(layer + 1)
            others(layer + 1)

    pltpu.make_async_copy(state, out_hbm, out_sem).wait()
    for copy in id_copies:
        copy.wait_send()
    for layer in range(LAYERS):
        wout_copies(layer)[1].wait_send()

    def drain(u, _):
        layer, h = u // here, lax.rem(u, here)
        wait(kv.at[u, pl.ds(0, 4)], kv_send.at[u, 0])
        wait(kv.at[u, 0], kv_send.at[u, 1])
        wait(kv.at[u, 2], kv_send.at[u, 2])
        wait(kv.at[u, 5], kv_send.at[u, 3])
        wait(qown.at[layer, h], q_send.at[layer, h])
        wait(psend.at[layer, h], p_send.at[layer, h])
        wait(psend.at[layer, h], z_send.at[layer, h])
        return 0

    lax.fori_loop(0, units, drain, 0)


def on_device(ring, cand_embed, cand_ids, hist_ids, hist_len, hist_keys, hist_values, w_in, w_out):
    count, width = cand_embed.shape[1:]
    local = w_in.shape[3]
    head = width // HEADS
    here = local // head
    rows = hist_ids.shape[1]
    units = LAYERS * here
    dma = pltpu.SemaphoreType.DMA
    any_space = pl.BlockSpec(memory_space=pl.ANY)
    out = pl.pallas_call(
        functools.partial(kernel, (ring, rows, here, width, head)),
        out_shape=jax.ShapeDtypeStruct((count, width), F32),
        in_specs=[pl.BlockSpec(memory_space=pltpu.SMEM)] + [any_space] * 7,
        out_specs=any_space,
        scratch_shapes=[
            pltpu.VMEM((units, 8, 2, rows, head), BF),
            pltpu.VMEM((LAYERS, here, count, head), BF),
            pltpu.VMEM((LAYERS, here, count, head), BF),
            pltpu.VMEM((LAYERS, here, count, head), BF),
            pltpu.VMEM((LAYERS, here, count, head), BF),
            pltpu.VMEM((LAYERS, count, width), BF),
            pltpu.VMEM((here, count, head), BF),
            pltpu.VMEM((here, count, head), BF),
            pltpu.VMEM((here, count, head), F32),
            pltpu.VMEM((LAYERS, 4, width, local), BF),
            pltpu.VMEM((LAYERS, width, width), BF),
            pltpu.VMEM((count, width), BF),
            pltpu.VMEM((count, width), F32),
            pltpu.VMEM((count, width), BF),
            pltpu.VMEM((2, 8, count, rows), BF),
            pltpu.VMEM((2, 1, count), jnp.int32),
            pltpu.VMEM((8, 1, rows), jnp.int32),
            pltpu.VMEM((2, count, head), F32),
            dma((units, 8)),
            dma((units, 4)),
            dma((LAYERS, here)),
            dma((LAYERS, here)),
            dma((LAYERS, here)),
            dma((LAYERS, here)),
            dma((LAYERS, here)),
            dma((LAYERS, here)),
            dma((LAYERS, 4)),
            dma((2 * LAYERS,)),
            dma((LAYERS,)),
            dma((9,)),
            dma((8,)),
            dma((3,)),
            dma,
        ],
        compiler_params=pltpu.CompilerParams(
            collective_id=0, has_side_effects=True, vmem_limit_bytes=60 * 1024 * 1024
        ),
        cost_estimate=pl.CostEstimate(
            flops=15 * 10**9, bytes_accessed=16 * 2**20, transcendentals=2 * 10**7
        ),
        name="hstu_layers",
    )(
        hist_len,
        cand_embed[0],
        cand_ids,
        hist_ids,
        hist_keys[0],
        hist_values[0],
        w_in.transpose(0, 2, 1, 3),
        w_out,
    )
    return out[None]


def solution(mesh):
    in_specs = (
        P("user", "cand", None),
        P("user", "cand"),
        P("user", ("cand", "tensor")),
        P("user"),
        P("user", None, ("cand", "tensor"), None),
        P("user", None, ("cand", "tensor"), None),
        P(None, None, None, "tensor"),
        P(None, "tensor", None),
    )
    out_specs = P("user", "cand", None)
    ring = mesh.shape["cand"] // 2
    return jax.shard_map(
        functools.partial(on_device, ring),
        mesh=mesh,
        in_specs=in_specs,
        out_specs=out_specs,
        check_vma=False,
    )
```

```python
import functools

import jax
import jax.numpy as jnp
from jax import lax
from jax.experimental import pallas as pl
from jax.experimental.pallas import tpu as pltpu
from jax.sharding import PartitionSpec as P

HEADS = 8
LAYERS = 2
BF = jnp.bfloat16
F32 = jnp.float32
SELF, LEFT, RIGHT, FAR = 0, 1, 2, 3


def gated(half):
    return half + half * jnp.tanh(half)


def kernel(
    dims,
    len_ref,
    embed_hbm,
    cid_hbm,
    hid_hbm,
    key_hbm,
    val_hbm,
    win_hbm,
    wout_hbm,
    out_hbm,
    kv,
    qown,
    qrem,
    psend,
    precv,
    zbuf,
    kown,
    vown,
    uown,
    raw,
    win,
    wout,
    embed,
    state,
    normed,
    mask,
    cids,
    hids,
    acc,
    kv_recv,
    kv_send,
    q_recv,
    q_send,
    p_recv,
    p_send,
    z_recv,
    z_send,
    w_sem,
    wo_sem,
    wo_recv,
    id_recv,
    id_send,
    loc_sem,
    out_sem,
):
    ring, rows, here, width, head = dims
    local = here * head
    count = state.shape[0]
    units = LAYERS * here
    scale = head ** (-0.5)

    cand = lax.axis_index("cand")
    t = lax.axis_index("tensor")
    y = lax.rem(cand, ring)
    plane = cand - y
    right = plane + lax.rem(y + 1, ring)
    left = plane + lax.rem(y + ring - 1, ring)
    far = plane + lax.rem(y + 2, ring)
    across = lax.rem(cand + ring, 2 * ring)

    peers = [(cand, 1 - t), (across, t)]
    for chip in (left, right, far):
        peers += [(chip, 0), (chip, 1)]

    embed_copy = pltpu.make_async_copy(embed_hbm, embed, loc_sem.at[0])
    embed_copy.start()

    def win_copy(layer):
        return pltpu.make_async_copy(win_hbm.at[layer], raw.at[layer], w_sem.at[layer])

    win_copy(0).start()

    barrier = pltpu.get_barrier_semaphore()
    for chip, core in peers:
        pl.semaphore_signal(barrier, inc=1, device_id={"cand": chip, "tensor": core})
    pl.semaphore_wait(barrier, len(peers))

    def remote(src, dst, send, recv, chip, core):
        return pltpu.make_async_remote_copy(
            src_ref=src,
            dst_ref=dst,
            send_sem=send,
            recv_sem=recv,
            device_id={"cand": chip, "tensor": core},
        )

    def wait(ref, sem):
        pltpu.make_async_copy(ref, ref, sem).wait()

    hid_local = pltpu.make_async_copy(hid_hbm, hids.at[SELF * 2 + t], loc_sem.at[1])
    cid_local = pltpu.make_async_copy(cid_hbm, cids.at[1], loc_sem.at[2])
    hid_local.start()
    cid_local.start()
    id_copies = [remote(cid_hbm, cids.at[0], id_send.at[0], id_recv.at[8], across, t)]
    targets = [
        (cand, 1 - t, SELF),
        (right, 0, LEFT),
        (right, 1, LEFT),
        (left, 0, RIGHT),
        (left, 1, RIGHT),
        (far, 0, FAR),
        (far, 1, FAR),
    ]
    for i, (chip, core, origin) in enumerate(targets):
        slot = origin * 2 + t
        id_copies.append(
            remote(hid_hbm, hids.at[slot], id_send.at[1 + i], id_recv.at[slot], chip, core)
        )
    for copy in id_copies:
        copy.start()

    def direct(u):
        layer, h = u // here, lax.rem(u, here)
        own = pl.ds(pl.multiple_of(t * local + h * head, head), head)
        other = pl.ds(pl.multiple_of((1 - t) * local + h * head, head), head)
        mine = SELF * 2 + t
        for i, src in enumerate((key_hbm, val_hbm)):
            for chip, origin in ((right, LEFT), (left, RIGHT)):
                slot = origin * 2 + t
                for core in (0, 1):
                    cols = pl.ds(core * local + pl.multiple_of(h * head, head), head)
                    remote(
                        src.at[layer, :, cols],
                        kv.at[u, i, slot],
                        kv_send.at[u, 0],
                        kv_recv.at[u, slot],
                        chip,
                        core,
                    ).start()
            remote(
                src.at[layer, :, other],
                kv.at[u, i, mine],
                kv_send.at[u, 1],
                kv_recv.at[u, mine],
                cand,
                1 - t,
            ).start()
            pltpu.make_async_copy(
                src.at[layer, :, own], kv.at[u, i, mine], kv_recv.at[u, mine]
            ).start()

    def forward(u):
        for slot, to, chip, k in ((2, 6, right, 2), (5, 7, left, 3)):
            wait(kv.at[u, :, slot], kv_recv.at[u, slot])
            remote(
                kv.at[u, :, slot], kv.at[u, :, to], kv_send.at[u, k], kv_recv.at[u, to], chip, t
            ).start()

    direct(0)
    direct(1)

    win_copy(1).start()

    own_half = pl.ds(pl.multiple_of(t * local, local), local)

    def wout_copies(layer):
        src, dst = wout_hbm.at[layer], wout.at[layer, own_half]
        return (
            pltpu.make_async_copy(src, dst, wo_sem.at[layer]),
            remote(src, dst, wo_sem.at[2 + layer], wo_recv.at[layer], cand, 1 - t),
        )

    def row_blocks(body, size):
        def step(i, _):
            body(pl.ds(pl.multiple_of(i * size, size), size))
            return 0

        lax.fori_loop(0, count // size, step, 0)

    def normalise(x):
        return (x * lax.rsqrt(jnp.mean(x * x, axis=-1, keepdims=True) + 1e-06)).astype(BF)

    embed_copy.wait()

    def first(block):
        x = embed[block, :].astype(F32)
        state[block, :] = x
        normed[block, :] = normalise(x)

    row_blocks(first, 128)

    def relay(layer):
        win_copy(layer).wait()

        def step(i, _):
            piece = pl.ds(pl.multiple_of(i * 64, 64), 64)
            win[layer, :, piece, :] = jnp.swapaxes(raw[layer, piece], 0, 1)
            return 0

        lax.fori_loop(0, width // 64, step, 0)

    def project(layer, j):
        s = jnp.dot(normed[...], win[layer, j], preferred_element_type=F32)
        return gated(0.5 * s)

    def split(ref, value):
        value = value.astype(ref.dtype)
        for h in range(here):
            ref[h] = value[:, h * head : (h + 1) * head]

    def queries(layer):
        split(qown.at[layer], project(layer, 2) * (0.5 * scale))
        for h in range(here):
            remote(
                qown.at[layer, h],
                qrem.at[layer, h],
                q_send.at[layer, h],
                q_recv.at[layer, h],
                across,
                t,
            ).start()

    def others(layer):
        for j, ref in ((3, kown), (1, vown), (0, uown)):
            split(ref, project(layer, j))

    relay(0)
    queries(0)
    forward(0)
    direct(2)
    others(0)

    for copies in (wout_copies(0), wout_copies(1)):
        for copy in copies:
            copy.start()
    relay(1)

    hid_local.wait()
    cid_local.wait()
    wait(cids.at[0], id_recv.at[8])
    wait(hids.at[SELF * 2 + 1 - t], id_recv.at[SELF * 2 + 1 - t])
    for slot in range(2, 8):
        wait(hids.at[slot], id_recv.at[slot])
    length = len_ref[0]
    for side in range(2):
        column = jnp.broadcast_to(cids[side].astype(F32), (128, count)).T

        def one_slot(slot, _, side=side, column=column):
            origin = slot // 2
            shift = jnp.where(origin == LEFT, ring - 1, jnp.where(origin == FAR, 2, 0))
            shift = jnp.where(origin == RIGHT, 1, shift)
            start = ((plane + lax.rem(y + shift, ring)) * 2 + lax.rem(slot, 2)) * rows
            for part in range(rows // 128):
                piece = slice(part * 128, (part + 1) * 128)
                where = pl.ds(pl.multiple_of(slot * rows + part * 128, 128), 128)
                ids = hids[slot, :, piece].astype(F32)
                at = start + part * 128 + lax.broadcasted_iota(jnp.int32, (1, 128), 1)
                live = jnp.where(at < length, 1.0, 0.0).astype(F32)
                mask[side, :, where] = jnp.where(column == ids, 0.0, live).astype(BF)
            return 0

        lax.fori_loop(0, 8, one_slot, 0)

    def attend(side, layer, h, u):
        q = (qrem, qown)[side][layer, h]
        keys = kv[u, 0].reshape(8 * rows, head)
        values = kv[u, 1].reshape(8 * rows, head)
        half = lax.dot_general(
            q, keys, (((1,), (1,)), ((), ())), preferred_element_type=F32
        )
        weights = gated(half).astype(BF) * mask[side]
        return jnp.dot(weights, values, preferred_element_type=F32)

    def finish(layer, h):
        wait(precv.at[layer, h], p_recv.at[layer, h])
        cols = pl.ds(pl.multiple_of(t * local + h * head, head), head)
        total = acc[h] + precv[layer, h].astype(F32)
        zbuf[layer, :, cols] = (total * uown[h]).astype(BF)
        remote(
            zbuf.at[layer, :, cols],
            zbuf.at[layer, :, cols],
            z_send.at[layer, h],
            z_recv.at[layer, h],
            cand,
            1 - t,
        ).start()

    for layer in range(LAYERS):

        def one_head(h, _, layer=layer):
            u = layer * here + h
            if layer == 0:
                forward(u + 1)
                direct(u + 3)
            else:

                @pl.when(h < 2)
                def _():
                    forward(u + 2)

            q = qown[layer, h].astype(F32)
            own = gated(jnp.sum(q * kown[h].astype(F32), axis=-1, keepdims=True))
            acc[h] = own * vown[h].astype(F32)
            wait(qrem.at[layer, h], q_recv.at[layer, h])
            for slot in (0, 1, 3, 4, 6, 7):
                wait(kv.at[u, :, slot], kv_recv.at[u, slot])
            psend[layer, h] = attend(0, layer, h, u).astype(BF)
            remote(
                psend.at[layer, h],
                precv.at[layer, h],
                p_send.at[layer, h],
                p_recv.at[layer, h],
                across,
                t,
            ).start()
            acc[h] += attend(1, layer, h, u)

            @pl.when(h > 0)
            def _():
                finish(layer, h - 1)

            return 0

        lax.fori_loop(0, here, one_head, 0)
        finish(layer, here - 1)

        if layer == 0:
            forward(here + 1)
            direct(here + 3)

        for copy in wout_copies(layer)[:1]:
            copy.wait()
        other_half = pl.ds(pl.multiple_of((1 - t) * local, local), local)
        wait(wout.at[layer, other_half], wo_recv.at[layer])
        for h in range(here):
            cols = pl.ds(pl.multiple_of((1 - t) * local, local) + h * head, head)
            wait(zbuf.at[layer, :, cols], z_recv.at[layer, h])

        def last(block, layer=layer):
            z = zbuf[layer, block, :]
            zf = z.astype(F32)
            size = lax.rsqrt(jnp.mean(zf * zf, axis=-1, keepdims=True) + 1e-06)
            x = state[block, :] + size * jnp.dot(z, wout[layer], preferred_element_type=F32)
            state[block, :] = x
            if layer + 1 < LAYERS:
                normed[block, :] = normalise(x)
            else:
                pltpu.make_async_copy(state.at[block], out_hbm.at[block], out_sem).start()

        row_blocks(last, 256)
        if layer + 1 < LAYERS:
            queries(layer + 1)
            others(layer + 1)

    pltpu.make_async_copy(state, out_hbm, out_sem).wait()
    for copy in id_copies:
        copy.wait_send()
    for layer in range(LAYERS):
        wout_copies(layer)[1].wait_send()

    def drain(u, _):
        layer, h = u // here, lax.rem(u, here)
        wait(kv.at[u, :, pl.ds(0, 4)], kv_send.at[u, 0])
        wait(kv.at[u, :, 0], kv_send.at[u, 1])
        wait(kv.at[u, :, 2], kv_send.at[u, 2])
        wait(kv.at[u, :, 5], kv_send.at[u, 3])
        wait(qown.at[layer, h], q_send.at[layer, h])
        wait(psend.at[layer, h], p_send.at[layer, h])
        wait(psend.at[layer, h], z_send.at[layer, h])
        return 0

    lax.fori_loop(0, units, drain, 0)


def on_device(ring, cand_embed, cand_ids, hist_ids, hist_len, hist_keys, hist_values, w_in, w_out):
    count, width = cand_embed.shape[1:]
    local = w_in.shape[3]
    head = width // HEADS
    here = local // head
    rows = hist_ids.shape[1]
    units = LAYERS * here
    dma = pltpu.SemaphoreType.DMA
    any_space = pl.BlockSpec(memory_space=pl.ANY)
    out = pl.pallas_call(
        functools.partial(kernel, (ring, rows, here, width, head)),
        out_shape=jax.ShapeDtypeStruct((count, width), F32),
        in_specs=[pl.BlockSpec(memory_space=pltpu.SMEM)] + [any_space] * 7,
        out_specs=any_space,
        scratch_shapes=[
            pltpu.VMEM((units, 2, 8, rows, head), BF),
            pltpu.VMEM((LAYERS, here, count, head), BF),
            pltpu.VMEM((LAYERS, here, count, head), BF),
            pltpu.VMEM((LAYERS, here, count, head), BF),
            pltpu.VMEM((LAYERS, here, count, head), BF),
            pltpu.VMEM((LAYERS, count, width), BF),
            pltpu.VMEM((here, count, head), BF),
            pltpu.VMEM((here, count, head), BF),
            pltpu.VMEM((here, count, head), F32),
            pltpu.VMEM((LAYERS, width, 4, local), BF),
            pltpu.VMEM((LAYERS, 4, width, local), BF),
            pltpu.VMEM((LAYERS, width, width), BF),
            pltpu.VMEM((count, width), BF),
            pltpu.VMEM((count, width), F32),
            pltpu.VMEM((count, width), BF),
            pltpu.VMEM((2, count, 8 * rows), BF),
            pltpu.VMEM((2, 1, count), jnp.int32),
            pltpu.VMEM((8, 1, rows), jnp.int32),
            pltpu.VMEM((here, count, head), F32),
            dma((units, 8)),
            dma((units, 4)),
            dma((LAYERS, here)),
            dma((LAYERS, here)),
            dma((LAYERS, here)),
            dma((LAYERS, here)),
            dma((LAYERS, here)),
            dma((LAYERS, here)),
            dma((LAYERS,)),
            dma((2 * LAYERS,)),
            dma((LAYERS,)),
            dma((9,)),
            dma((8,)),
            dma((3,)),
            dma,
        ],
        compiler_params=pltpu.CompilerParams(
            collective_id=0, has_side_effects=True, vmem_limit_bytes=60 * 1024 * 1024
        ),
        cost_estimate=pl.CostEstimate(
            flops=15 * 10**9, bytes_accessed=16 * 2**20, transcendentals=2 * 10**7
        ),
        name="hstu_layers",
    )(
        hist_len,
        cand_embed[0],
        cand_ids,
        hist_ids,
        hist_keys[0],
        hist_values[0],
        w_in,
        w_out,
    )
    return out[None]


def solution(mesh):
    in_specs = (
        P("user", "cand", None),
        P("user", "cand"),
        P("user", ("cand", "tensor")),
        P("user"),
        P("user", None, ("cand", "tensor"), None),
        P("user", None, ("cand", "tensor"), None),
        P(None, None, None, "tensor"),
        P(None, "tensor", None),
    )
    out_specs = P("user", "cand", None)
    ring = mesh.shape["cand"] // 2
    return jax.shard_map(
        functools.partial(on_device, ring),
        mesh=mesh,
        in_specs=in_specs,
        out_specs=out_specs,
        check_vma=False,
    )
```

```python
import functools

import jax
import jax.numpy as jnp
from jax import lax
from jax.experimental import pallas as pl
from jax.experimental.pallas import tpu as pltpu
from jax.sharding import PartitionSpec as P

HEADS = 8
LAYERS = 2
BF = jnp.bfloat16
F32 = jnp.float32


def gated(half):
    return half + half * jnp.tanh(half)


def kernel(
    dims,
    len_ref,
    embed_hbm,
    cid_hbm,
    hid_hbm,
    key_hbm,
    val_hbm,
    win_hbm,
    wout_hbm,
    z_hbm,
    state_hbm,
    wout_full_hbm,
    kv,
    qown,
    qrem,
    psend,
    precv,
    zbuf,
    kown,
    vown,
    uown,
    raw,
    win,
    wout,
    embed,
    state,
    normed,
    mask,
    cids,
    hids,
    acc,
    kv_recv,
    kv_send,
    q_recv,
    q_send,
    p_recv,
    p_send,
    z_recv,
    z_send,
    zl_sem,
    w_sem,
    wo_sem,
    wo_recv,
    cid_recv,
    hid_recv,
    id_send,
    loc_sem,
    out_sem,
):
    ring, rows, here, width, head = dims
    local = here * head
    count = state.shape[0]
    units = LAYERS * here
    scale = head ** (-0.5)

    cand = lax.axis_index("cand")
    t = lax.axis_index("tensor")
    y = lax.rem(cand, ring)
    plane = cand - y
    right = plane + lax.rem(y + 1, ring)
    left = plane + lax.rem(y + ring - 1, ring)
    far = plane + lax.rem(y + 2, ring)
    across = lax.rem(cand + ring, 2 * ring)
    near = y + 1 - 2 * lax.rem(y, 2)
    pairs = (plane + near, plane + ring - 1 - y)
    diagonals = (ring - plane + near, 2 * ring - 1 - plane - y)

    def roles(h):
        ringed, second = h % 2 if isinstance(h, int) else lax.rem(h, 2), h // 2
        block = 1 - ringed
        pair = (1 - second) * pairs[0] + second * pairs[1]
        outer = (1 - second) * pairs[1] + second * pairs[0]
        diagonal = (1 - second) * diagonals[0] + second * diagonals[1]
        return dict(
            first=ringed * right + block * across,
            other=ringed * left + block * pair,
            first_on=ringed * right + block * pair,
            other_on=ringed * left + block * across,
            partner=ringed * across + block * outer,
            origins=(
                cand,
                ringed * left + block * across,
                ringed * right + block * pair,
                ringed * far + block * diagonal,
            ),
            partner_ids=ringed * 1 + block * (3 - second),
            kind=block * (1 + second),
        )

    peers = [(cand, 1 - t)]
    for chip in (left, right, across, far, *diagonals):
        peers += [(chip, 0), (chip, 1)]

    embed_copy = pltpu.make_async_copy(embed_hbm, embed, loc_sem.at[0])
    embed_copy.start()

    def win_copy(layer):
        return pltpu.make_async_copy(win_hbm.at[layer], raw, w_sem.at[layer])

    win_copy(0).start()

    barrier = pltpu.get_barrier_semaphore()
    for chip, core in peers:
        pl.semaphore_signal(barrier, inc=1, device_id={"cand": chip, "tensor": core})
    pl.semaphore_wait(barrier, len(peers))

    def remote(src, dst, send, recv, chip, core):
        return pltpu.make_async_remote_copy(
            src_ref=src,
            dst_ref=dst,
            send_sem=send,
            recv_sem=recv,
            device_id={"cand": chip, "tensor": core},
        )

    def wait(ref, sem):
        pltpu.make_async_copy(ref, ref, sem).wait()

    row = cand * 2 + t
    hid_local = pltpu.make_async_copy(hid_hbm, hids.at[row], loc_sem.at[1])
    cid_local = pltpu.make_async_copy(cid_hbm, cids.at[0], loc_sem.at[2])
    id_copies = []
    for i, chip in enumerate((across, *pairs)):
        id_copies.append(
            remote(cid_hbm, cids.at[1 + i], id_send.at[i], cid_recv.at[i], chip, t)
        )
    for i, (chip, core) in enumerate(peers):
        id_copies.append(
            remote(hid_hbm, hids.at[row], id_send.at[3 + i], hid_recv.at[row], chip, core)
        )

    def direct(u):
        layer, h = u // here, lax.rem(u, here)
        own = pl.ds(pl.multiple_of(t * local + h * head, head), head)
        other = pl.ds(pl.multiple_of((1 - t) * local + h * head, head), head)
        role = roles(h)
        for i, src in enumerate((key_hbm, val_hbm)):
            for chip, slot in ((role["first"], 2 + t), (role["other"], 4 + t)):
                for core in (0, 1):
                    cols = pl.ds(core * local + pl.multiple_of(h * head, head), head)
                    remote(
                        src.at[layer, :, cols],
                        kv.at[u, i, slot],
                        kv_send.at[u, 0],
                        kv_recv.at[u, slot],
                        chip,
                        core,
                    ).start()
            remote(
                src.at[layer, :, other],
                kv.at[u, i, t],
                kv_send.at[u, 1],
                kv_recv.at[u, t],
                cand,
                1 - t,
            ).start()
            pltpu.make_async_copy(
                src.at[layer, :, own], kv.at[u, i, t], kv_recv.at[u, t]
            ).start()

    def forward(u):
        role = roles(lax.rem(u, here))
        for slot, to, chip, k in ((2, 6, role["first_on"], 2), (5, 7, role["other_on"], 3)):
            wait(kv.at[u, :, slot], kv_recv.at[u, slot])
            remote(
                kv.at[u, :, slot], kv.at[u, :, to], kv_send.at[u, k], kv_recv.at[u, to], chip, t
            ).start()

    direct(0)
    direct(1)
    hid_local.start()
    cid_local.start()
    for copy in id_copies:
        copy.start()

    own_half = pl.ds(pl.multiple_of(t * local, local), local)

    def wout_copies(layer):
        src, dst = wout_hbm.at[layer], wout.at[layer, own_half]
        return (
            pltpu.make_async_copy(src, dst, wo_sem.at[layer]),
            remote(src, dst, wo_sem.at[2 + layer], wo_recv.at[layer], cand, 1 - t),
        )

    def row_blocks(body, size):
        def step(i, _):
            body(pl.ds(pl.multiple_of(i * size, size), size))
            return 0

        lax.fori_loop(0, count // size, step, 0)

    def normalise(x):
        return (x * lax.rsqrt(jnp.mean(x * x, axis=-1, keepdims=True) + 1e-06)).astype(BF)

    embed_copy.wait()

    def first(block):
        x = embed[block, :].astype(F32)
        state[block, :] = x
        normed[block, :] = normalise(x)

    row_blocks(first, 128)

    def relay(layer):
        win_copy(layer).wait()

        def step(i, _):
            piece = pl.ds(pl.multiple_of(i * 64, 64), 64)
            win[:, piece, :] = jnp.swapaxes(raw[piece], 0, 1)
            return 0

        lax.fori_loop(0, width // 64, step, 0)

    def project(j):
        s = jnp.dot(normed[...], win[j], preferred_element_type=F32)
        return gated(0.5 * s)

    def split(ref, value):
        value = value.astype(ref.dtype)
        for h in range(here):
            ref[h] = value[:, h * head : (h + 1) * head]

    def queries(layer):
        split(qown.at[layer], project(2) * (0.5 * scale))
        for h in range(here):
            remote(
                qown.at[layer, h],
                qrem.at[layer, h],
                q_send.at[layer, h],
                q_recv.at[layer, h],
                roles(h)["partner"],
                t,
            ).start()

    def others():
        for j, ref in ((3, kown), (1, vown), (0, uown)):
            split(ref, project(j))

    relay(0)
    win_copy(1).start()
    queries(0)
    direct(2)
    others()
    forward(0)

    for copies in (wout_copies(0), wout_copies(1)):
        for copy in copies:
            copy.start()
    relay(1)

    hid_local.wait()
    cid_local.wait()
    for i in range(3):
        wait(cids.at[1 + i], cid_recv.at[i])
    for chip, core in peers:
        wait(hids.at[chip * 2 + core], hid_recv.at[chip * 2 + core])
    length = len_ref[0]

    def build_mask(h):
        role = roles(h)
        kind = role["kind"]
        for side in range(2):
            line = (role["partner_ids"], 0)[side]
            column = jnp.broadcast_to(cids[line].astype(F32), (128, count)).T
            for origin, chip in enumerate(role["origins"]):

                def one_core(core, _, side=side, column=column, origin=origin, chip=chip):
                    for part in range(rows // 128):
                        start = (chip * 2 + core) * rows + part * 128
                        at = start + lax.broadcasted_iota(jnp.int32, (1, 128), 1)
                        live = jnp.where(at < length, 1.0, 0.0).astype(F32)
                        piece = slice(part * 128, (part + 1) * 128)
                        ids = hids[chip * 2 + core, :, piece].astype(F32)
                        to = (origin * 2 + core) * rows + part * 128
                        to = pl.ds(pl.multiple_of(to, 128), 128)
                        mask[kind, side, :, to] = jnp.where(column == ids, 0.0, live).astype(BF)
                    return 0

                lax.fori_loop(0, 2, one_core, 0)

    def attend(side, layer, h, u):
        q = (qrem, qown)[side][layer, h]
        keys = kv[u, 0].reshape(8 * rows, head)
        values = kv[u, 1].reshape(8 * rows, head)
        half = lax.dot_general(
            q, keys, (((1,), (1,)), ((), ())), preferred_element_type=F32
        )
        weights = gated(half).astype(BF) * mask[roles(h)["kind"], side]
        return jnp.dot(weights, values, preferred_element_type=F32)

    def finish(layer, h):
        wait(precv.at[layer, h], p_recv.at[layer, h])
        cols = pl.ds(pl.multiple_of(t * local + h * head, head), head)
        total = acc[h] + precv[layer, h].astype(F32)
        zbuf[layer, :, cols] = (total * uown[h]).astype(BF)
        if layer + 1 == LAYERS:
            to = z_hbm.at[:, cols]
            pltpu.make_async_copy(zbuf.at[layer, :, cols], to, zl_sem.at[h]).start()
        else:
            to = zbuf.at[layer, :, cols]
        remote(
            zbuf.at[layer, :, cols],
            to,
            z_send.at[layer, h],
            z_recv.at[layer, h],
            cand,
            1 - t,
        ).start()

    other_half = pl.ds(pl.multiple_of((1 - t) * local, local), local)
    result_copies = (
        pltpu.make_async_copy(state, state_hbm, out_sem.at[0]),
        pltpu.make_async_copy(wout.at[LAYERS - 1], wout_full_hbm, out_sem.at[1]),
    )
    for layer in range(LAYERS):

        def one_head(h, _, layer=layer):
            u = layer * here + h
            if layer == 0:
                forward(u + 1)
                direct(u + 3)

                @pl.when(h < 3)
                def _():
                    build_mask(h)

            else:

                @pl.when(h < 2)
                def _():
                    forward(u + 2)

            q = qown[layer, h].astype(F32)
            own = gated(jnp.sum(q * kown[h].astype(F32), axis=-1, keepdims=True))
            acc[h] = own * vown[h].astype(F32)
            wait(qrem.at[layer, h], q_recv.at[layer, h])
            for slot in (0, 1, 3, 4, 6, 7):
                wait(kv.at[u, :, slot], kv_recv.at[u, slot])
            psend[layer, h] = attend(0, layer, h, u).astype(BF)
            remote(
                psend.at[layer, h],
                precv.at[layer, h],
                p_send.at[layer, h],
                p_recv.at[layer, h],
                roles(h)["partner"],
                t,
            ).start()
            acc[h] += attend(1, layer, h, u)

            @pl.when(h > 0)
            def _():
                finish(layer, h - 1)

            return 0

        lax.fori_loop(0, here, one_head, 0)
        if layer == 0:
            forward(here + 1)
            direct(here + 3)
        finish(layer, here - 1)
        if layer + 1 == LAYERS:
            break

        wout_copies(layer)[0].wait()
        wait(wout.at[layer, other_half], wo_recv.at[layer])
        for h in range(here):
            cols = pl.ds(pl.multiple_of((1 - t) * local, local) + h * head, head)
            wait(zbuf.at[layer, :, cols], z_recv.at[layer, h])

        def last(block, layer=layer):
            z = zbuf[layer, block, :]
            zf = z.astype(F32)
            size = lax.rsqrt(jnp.mean(zf * zf, axis=-1, keepdims=True) + 1e-06)
            x = state[block, :] + size * jnp.dot(z, wout[layer], preferred_element_type=F32)
            state[block, :] = x
            normed[block, :] = normalise(x)

        row_blocks(last, 256)
        queries(layer + 1)
        others()
        wout_copies(layer + 1)[0].wait()
        wait(wout.at[layer + 1, other_half], wo_recv.at[layer + 1])
        for copy in result_copies:
            copy.start()

    for copy in result_copies:
        copy.wait()
    for h in range(here):
        cols = pl.ds(pl.multiple_of(t * local, local) + h * head, head)
        pltpu.make_async_copy(zbuf.at[LAYERS - 1, :, cols], z_hbm.at[:, cols], zl_sem.at[h]).wait()
        cols = pl.ds(pl.multiple_of((1 - t) * local, local) + h * head, head)
        wait(z_hbm.at[:, cols], z_recv.at[LAYERS - 1, h])
    for copy in id_copies:
        copy.wait_send()
    for layer in range(LAYERS):
        wout_copies(layer)[1].wait_send()

    def drain(u, _):
        layer, h = u // here, lax.rem(u, here)
        wait(kv.at[u, :, pl.ds(0, 4)], kv_send.at[u, 0])
        wait(kv.at[u, :, 0], kv_send.at[u, 1])
        wait(kv.at[u, :, 2], kv_send.at[u, 2])
        wait(kv.at[u, :, 5], kv_send.at[u, 3])
        wait(qown.at[layer, h], q_send.at[layer, h])
        wait(psend.at[layer, h], p_send.at[layer, h])
        wait(psend.at[layer, h], z_send.at[layer, h])
        return 0

    lax.fori_loop(0, units, drain, 0)


def project_out(z_ref, state_ref, w_ref, out_ref, size):
    @pl.when(pl.program_id(0) == 0)
    def _():
        zf = z_ref[...].astype(F32)
        size[...] = lax.rsqrt(jnp.mean(zf * zf, axis=-1, keepdims=True) + 1e-06)

    product = jnp.dot(z_ref[...], w_ref[...], preferred_element_type=F32)
    out_ref[...] = state_ref[...] + size[...] * product


def on_device(ring, cand_embed, cand_ids, hist_ids, hist_len, hist_keys, hist_values, w_in, w_out):
    count, width = cand_embed.shape[1:]
    local = w_in.shape[3]
    head = width // HEADS
    here = local // head
    rows = hist_ids.shape[1]
    units = LAYERS * here
    dma = pltpu.SemaphoreType.DMA
    any_space = pl.BlockSpec(memory_space=pl.ANY)
    z, state, weights = pl.pallas_call(
        functools.partial(kernel, (ring, rows, here, width, head)),
        out_shape=(
            jax.ShapeDtypeStruct((count, width), BF),
            jax.ShapeDtypeStruct((count, width), F32),
            jax.ShapeDtypeStruct((width, width), BF),
        ),
        in_specs=[pl.BlockSpec(memory_space=pltpu.SMEM)] + [any_space] * 7,
        out_specs=(any_space,) * 3,
        scratch_shapes=[
            pltpu.VMEM((units, 2, 8, rows, head), BF),
            pltpu.VMEM((LAYERS, here, count, head), BF),
            pltpu.VMEM((LAYERS, here, count, head), BF),
            pltpu.VMEM((LAYERS, here, count, head), BF),
            pltpu.VMEM((LAYERS, here, count, head), BF),
            pltpu.VMEM((LAYERS, count, width), BF),
            pltpu.VMEM((here, count, head), BF),
            pltpu.VMEM((here, count, head), BF),
            pltpu.VMEM((here, count, head), F32),
            pltpu.VMEM((width, 4, local), BF),
            pltpu.VMEM((4, width, local), BF),
            pltpu.VMEM((LAYERS, width, width), BF),
            pltpu.VMEM((count, width), BF),
            pltpu.VMEM((count, width), F32),
            pltpu.VMEM((count, width), BF),
            pltpu.VMEM((3, 2, count, 8 * rows), BF),
            pltpu.VMEM((4, 1, count), jnp.int32),
            pltpu.VMEM((4 * ring, 1, rows), jnp.int32),
            pltpu.VMEM((here, count, head), F32),
            dma((units, 8)),
            dma((units, 4)),
            dma((LAYERS, here)),
            dma((LAYERS, here)),
            dma((LAYERS, here)),
            dma((LAYERS, here)),
            dma((LAYERS, here)),
            dma((LAYERS, here)),
            dma((here,)),
            dma((LAYERS,)),
            dma((2 * LAYERS,)),
            dma((LAYERS,)),
            dma((3,)),
            dma((4 * ring,)),
            dma((16,)),
            dma((3,)),
            dma((2,)),
        ],
        compiler_params=pltpu.CompilerParams(
            collective_id=0, has_side_effects=True, vmem_limit_bytes=60 * 1024 * 1024
        ),
        cost_estimate=pl.CostEstimate(
            flops=15 * 10**9, bytes_accessed=16 * 2**20, transcendentals=2 * 10**7
        ),
        name="hstu_layers",
    )(
        hist_len,
        cand_embed[0],
        cand_ids,
        hist_ids,
        hist_keys[0],
        hist_values[0],
        w_in,
        w_out,
    )
    step = min(256, width)
    return pl.pallas_call(
        project_out,
        grid=(width // step,),
        out_shape=jax.ShapeDtypeStruct((count, width), F32),
        in_specs=[
            pl.BlockSpec((count, width), lambda i: (0, 0)),
            pl.BlockSpec((count, step), lambda i: (0, i)),
            pl.BlockSpec((width, step), lambda i: (0, i)),
        ],
        out_specs=pl.BlockSpec((count, step), lambda i: (0, i)),
        scratch_shapes=[pltpu.VMEM((count, 1), F32)],
        compiler_params=pltpu.CompilerParams(vmem_limit_bytes=60 * 1024 * 1024),
        name="project_out",
    )(z, state, weights)[None]


def solution(mesh):
    in_specs = (
        P("user", "cand", None),
        P("user", "cand"),
        P("user", ("cand", "tensor")),
        P("user"),
        P("user", None, ("cand", "tensor"), None),
        P("user", None, ("cand", "tensor"), None),
        P(None, None, None, "tensor"),
        P(None, "tensor", None),
    )
    out_specs = P("user", "cand", None)
    ring = mesh.shape["cand"] // 2
    return jax.shard_map(
        functools.partial(on_device, ring),
        mesh=mesh,
        in_specs=in_specs,
        out_specs=out_specs,
        check_vma=False,
    )
```

```python
import functools

import jax
import jax.numpy as jnp
from jax import lax
from jax.experimental import pallas as pl
from jax.experimental.pallas import tpu as pltpu
from jax.sharding import PartitionSpec as P

HEADS = 8
LAYERS = 2
BF = jnp.bfloat16
KINDS = "RBARARBA"
OWN_FIRST = (0, 0)
ORDER = {
    "start": [(0, 1), (0, 0), (1, 0)],
    "o": [(1, 2)],
    "mask0": [(1, 1), (3, 0)],
    "mask1": [(2, 0), (0, 2), (0, 3)],
    ("s", 0): [(2, 1), (3, 1), (3, 2)],
    ("m", 0): [(1, 3)],
    ("n", 0): [(2, 2)],
    ("n", 1): [(0, 4), (2, 3)],
    ("n", 2): [(3, 3)],
    ("s", 3): [(0, 7), (1, 4), (1, 6)],
    ("n", 3): [(1, 5)],
    "t": [(2, 4), (0, 5), (3, 4)],
    ("s", 4): [(2, 5), (0, 6), (3, 5)],
    ("m", 4): [(3, 6)],
    ("n", 4): [(1, 7)],
    ("s", 5): [(2, 6), (2, 7)],
    ("s", 6): [(3, 7)],
}
F32 = jnp.float32


def gated(half):
    return half + half * jnp.tanh(half)


def kernel(
    dims,
    len_ref,
    embed_hbm,
    cid_hbm,
    hid_hbm,
    key_hbm,
    val_hbm,
    win_hbm,
    wout_hbm,
    out_hbm,
    kv,
    qown,
    qrem,
    psend,
    precv,
    zbuf,
    kown,
    vown,
    uown,
    raw,
    win,
    wout,
    embed,
    state,
    normed,
    mask,
    cids,
    hids,
    acc,
    base,
    squares,
    kv_recv,
    kv_send,
    q_recv,
    q_send,
    p_recv,
    p_send,
    z_recv,
    z_send,
    w_sem,
    wo_sem,
    wo_recv,
    cid_recv,
    hid_recv,
    id_send,
    loc_sem,
    out_sem,
):
    ring, rows, here, width, head = dims
    local = here * head
    count = state.shape[0]
    units = LAYERS * here
    scale = head ** (-0.5)

    cand = lax.axis_index("cand")
    t = lax.axis_index("tensor")
    y = lax.rem(cand, ring)
    plane = cand - y
    right = plane + lax.rem(y + 1, ring)
    left = plane + lax.rem(y + ring - 1, ring)
    far = plane + lax.rem(y + 2, ring)
    across = lax.rem(cand + ring, 2 * ring)
    near = y + 1 - 2 * lax.rem(y, 2)
    pairs = (plane + near, plane + ring - 1 - y)
    diagonals = (ring - plane + near, 2 * ring - 1 - plane - y)

    def roles(u):
        ringed = KINDS[u] == "R"
        pair, outer = pairs if KINDS[u] == "A" else pairs[::-1]
        diagonal = diagonals[0 if KINDS[u] == "A" else 1]
        return dict(
            first=pairs[0] if ringed else across,
            other=pairs[1] if ringed else pair,
            first_on=pairs[1] if ringed else pair,
            other_on=pairs[0] if ringed else across,
            partner=across if ringed else outer,
            origins=(cand, *pairs, far) if ringed else (cand, across, pair, diagonal),
            partner_ids={"R": 1, "A": 3, "B": 2}[KINDS[u]],
        )

    peers = [(cand, 1 - t)]
    for chip in (left, right, across, far, *diagonals):
        peers += [(chip, 0), (chip, 1)]

    embed_copy = pltpu.make_async_copy(embed_hbm, embed, loc_sem.at[0])
    embed_copy.start()

    def win_copy(layer):
        return pltpu.make_async_copy(win_hbm.at[layer], raw, w_sem.at[layer])

    win_copy(0).start()

    barrier = pltpu.get_barrier_semaphore()
    for chip, core in peers:
        pl.semaphore_signal(barrier, inc=1, device_id={"cand": chip, "tensor": core})
    pl.semaphore_wait(barrier, len(peers))

    def remote(src, dst, send, recv, chip, core):
        return pltpu.make_async_remote_copy(
            src_ref=src,
            dst_ref=dst,
            send_sem=send,
            recv_sem=recv,
            device_id={"cand": chip, "tensor": core},
        )

    def wait(ref, sem):
        pltpu.make_async_copy(ref, ref, sem).wait()

    row = cand * 2 + t
    hid_local = pltpu.make_async_copy(hid_hbm, hids.at[row], loc_sem.at[1])
    cid_local = pltpu.make_async_copy(cid_hbm, cids.at[0], loc_sem.at[2])
    id_copies = []
    for i, chip in enumerate((across, *pairs)):
        id_copies.append(
            remote(cid_hbm, cids.at[1 + i], id_send.at[i], cid_recv.at[i], chip, t)
        )
    for i, (chip, core) in enumerate(peers):
        id_copies.append(
            remote(hid_hbm, hids.at[row], id_send.at[3 + i], hid_recv.at[row], chip, core)
        )

    def direct(u, k):
        layer, h = u // here, u % here
        own = pl.ds(pl.multiple_of(t * local + h * head, head), head)
        other = pl.ds(pl.multiple_of((1 - t) * local + h * head, head), head)
        chip, slot = (roles(u)["first"], 2 + t) if k == 0 else (roles(u)["other"], 4 + t)
        for i, src in enumerate((key_hbm, val_hbm)):
            for core in (0, 1):
                cols = pl.ds(core * local + h * head, head)
                remote(
                    src.at[layer, :, cols],
                    kv.at[u, i, slot],
                    kv_send.at[u, k],
                    kv_recv.at[u, slot],
                    chip,
                    core,
                ).start()
            if k == 1:
                remote(
                    src.at[layer, :, other],
                    kv.at[u, i, t],
                    kv_send.at[u, 4],
                    kv_recv.at[u, t],
                    cand,
                    1 - t,
                ).start()
                pltpu.make_async_copy(
                    src.at[layer, :, own], kv.at[u, i, t], kv_recv.at[u, t]
                ).start()

    def forward(u, k):
        slot, to = ((2, 6), (5, 7))[k]
        chip = roles(u)[("first_on", "other_on")[k]]
        wait(kv.at[u, :, slot], kv_recv.at[u, slot])
        remote(
            kv.at[u, :, slot], kv.at[u, :, to], kv_send.at[u, 2 + k], kv_recv.at[u, to], chip, t
        ).start()

    def point(name):
        for step, u in ORDER.get(name, ()):
            (direct if step < 2 else forward)(u, step % 2)

    def unit_point(name, layer, h):
        for i in range(here - 1):
            if (name, layer * here + i) in ORDER:

                @pl.when(h == i)
                def _(i=i):
                    point((name, layer * here + i))

    point("start")
    hid_local.start()
    cid_local.start()
    for copy in id_copies:
        copy.start()

    def wout_copies(layer):
        copies = []
        for h in range(here):
            src = wout_hbm.at[layer, pl.ds(h * head, head)]
            dst = wout.at[layer, pl.ds(pl.multiple_of((h * 2 + t) * head, head), head)]
            copies += [
                pltpu.make_async_copy(src, dst, wo_sem.at[layer]),
                remote(src, dst, wo_sem.at[2 + layer], wo_recv.at[layer], cand, 1 - t),
            ]
        return copies

    def row_blocks(body, size):
        def step(i, _):
            body(pl.ds(pl.multiple_of(i * size, size), size))
            return 0

        lax.fori_loop(0, count // size, step, 0)

    def normalise(x):
        return (x * lax.rsqrt(jnp.mean(x * x, axis=-1, keepdims=True) + 1e-06)).astype(BF)

    embed_copy.wait()

    def first(block):
        x = embed[block, :].astype(F32)
        state[block, :] = x
        normed[block, :] = normalise(x)

    row_blocks(first, 128)

    def relay(layer):
        win_copy(layer).wait()

        def step(i, _):
            piece = pl.ds(pl.multiple_of(i * 64, 64), 64)
            win[:, piece, :] = jnp.swapaxes(raw[piece], 0, 1)
            return 0

        lax.fori_loop(0, width // 64, step, 0)

    def project(j):
        s = jnp.dot(normed[...], win[j], preferred_element_type=F32)
        return gated(0.5 * s)

    def split(ref, value):
        value = value.astype(ref.dtype)
        for h in range(here):
            ref[h] = value[:, h * head : (h + 1) * head]

    def queries(layer):
        split(qown.at[layer], project(2) * (0.5 * scale))
        for h in range(here):
            remote(
                qown.at[layer, h],
                qrem.at[layer, h],
                q_send.at[layer, h],
                q_recv.at[layer, h],
                roles(layer * here + h)["partner"],
                t,
            ).start()

    def others():
        for j, ref in ((3, kown), (1, vown), (0, uown)):
            split(ref, project(j))

    relay(0)
    win_copy(1).start()
    queries(0)
    point("q")
    others()
    point("o")

    for copies in (wout_copies(0), wout_copies(1)):
        for copy in copies:
            copy.start()
    relay(1)

    hid_local.wait()
    cid_local.wait()
    for i in range(3):
        wait(cids.at[1 + i], cid_recv.at[i])
    for chip, core in peers:
        wait(hids.at[chip * 2 + core], hid_recv.at[chip * 2 + core])
    length = len_ref[0]

    def build_mask(kind):
        role = roles(KINDS.index("RAB"[kind]))
        for side in range(2):
            line = (role["partner_ids"], 0)[side]
            column = jnp.broadcast_to(cids[line].astype(F32), (128, count)).T
            for origin, chip in enumerate(role["origins"]):

                def one_core(core, _, side=side, column=column, origin=origin, chip=chip):
                    for part in range(rows // 128):
                        start = (chip * 2 + core) * rows + part * 128
                        at = start + lax.broadcasted_iota(jnp.int32, (1, 128), 1)
                        live = jnp.where(at < length, 1.0, 0.0).astype(F32)
                        piece = slice(part * 128, (part + 1) * 128)
                        ids = hids[chip * 2 + core, :, piece].astype(F32)
                        to = (origin * 2 + core) * rows + part * 128
                        to = pl.ds(pl.multiple_of(to, 128), 128)
                        mask[kind, side, :, to] = jnp.where(column == ids, 0.0, live).astype(BF)
                    return 0

                lax.fori_loop(0, 2, one_core, 0)

    for i, kind in enumerate(dict.fromkeys(KINDS)):
        build_mask("RAB".index(kind))
        point(f"mask{i}")

    half_rows = [pl.ds(i * (count // 2), count // 2) for i in range(2)]
    all_rows = pl.ds(0, count)
    final = here - 1
    early = 2 * head * final

    def pick(values, h):
        result = jnp.int32(values[0])
        for i in range(1, len(values)):
            result = jnp.where(h == i, values[i], result)
        return result

    def attend(side, layer, h, u, kind, block):
        q = (qrem, qown)[side][layer, h, block, :]
        keys = kv[u, 0].reshape(8 * rows, head)
        values = kv[u, 1].reshape(8 * rows, head)
        half = lax.dot_general(
            q, keys, (((1,), (1,)), ((), ())), preferred_element_type=F32
        )
        weights = gated(half).astype(BF) * mask[kind, side, block, :]
        return jnp.dot(weights, values, preferred_element_type=F32)

    def send_part(layer, h, block, k):
        remote(
            psend.at[layer, h, block],
            precv.at[layer, h, block],
            p_send.at[layer, k],
            p_recv.at[layer, k],
            roles(layer * here + h)["partner"],
            t,
        ).start()

    def finish(layer, h, block, k):
        wait(precv.at[layer, h, block], p_recv.at[layer, k])
        q = qown[layer, h, block, :].astype(F32)
        own = gated(jnp.sum(q * kown[h, block, :].astype(F32), axis=-1, keepdims=True))
        total = acc[h, block, :] + precv[layer, h, block, :].astype(F32)
        total = (total + own * vown[h, block, :].astype(F32)) * uown[h, block, :]
        cols = pl.ds(pl.multiple_of((h * 2 + t) * head, head), head)
        zbuf[layer, block, cols] = total.astype(BF)
        remote(
            zbuf.at[layer, block, cols],
            zbuf.at[layer, block, cols],
            z_send.at[layer, k],
            z_recv.at[layer, k],
            cand,
            1 - t,
        ).start()

    def wait_z(layer, h, block, k):
        cols = pl.ds(pl.multiple_of((h * 2 + 1 - t) * head, head), head)
        wait(zbuf.at[layer, block, cols], z_recv.at[layer, k])

    def wait_kv(u):
        for slot in (0, 1, 3, 4, 6, 7):
            wait(kv.at[u, :, slot], kv_recv.at[u, slot])

    for layer in range(LAYERS):
        kinds = ["RAB".index(kind) for kind in KINDS[layer * here : (layer + 1) * here]]

        def one_head(h, _, layer=layer, kinds=kinds):
            u = layer * here + h
            unit_point("s", layer, h)
            wait_kv(u)
            kind = pick(kinds[:final], h)
            for i in range(2):
                side = i ^ OWN_FIRST[layer]
                if side == 0:
                    wait(qrem.at[layer, h], q_recv.at[layer, h])
                if i == 0:
                    unit_point("m", layer, h)
                if side == 0:
                    psend[layer, h] = attend(0, layer, h, u, kind, all_rows).astype(BF)
                    for j in range(final):

                        @pl.when(h == j)
                        def _(j=j):
                            send_part(layer, j, all_rows, j)

                else:
                    acc[h] = attend(1, layer, h, u, kind, all_rows)
                if i == 0:
                    if layer > 0:
                        pl.when(h == 0)(others)
                    unit_point("n", layer, h)

            @pl.when(h > 0)
            def _():
                finish(layer, h - 1, all_rows, h - 1)

            return 0

        lax.fori_loop(0, final, one_head, 0)

        u = layer * here + final
        point(("s", u))
        wait_kv(u)
        wait(qrem.at[layer, final], q_recv.at[layer, final])
        point(("m", u))
        for i, block in enumerate(half_rows):
            psend[layer, final, block, :] = attend(0, layer, final, u, kinds[-1], block).astype(BF)
            send_part(layer, final, block, final + i)
        point(("n", u))
        finish(layer, final - 1, all_rows, final - 1)
        acc[final] = attend(1, layer, final, u, kinds[-1], all_rows)
        if layer == 0:
            point("t")
        wait(wout.at[layer, pl.ds(0, local)], wo_sem.at[layer])
        wait(wout.at[layer, pl.ds(0, local)], wo_recv.at[layer])
        for h in range(final):
            wait_z(layer, h, all_rows, h)
        z = zbuf[layer, :, :early]
        zf = z.astype(F32)
        squares[...] = jnp.sum(zf * zf, axis=-1, keepdims=True)
        base[...] = jnp.dot(z, wout[layer, :early, :], preferred_element_type=F32)
        for i, block in enumerate(half_rows):
            finish(layer, final, block, final + i)
        if layer == 0:
            point("w")
        for i, block in enumerate(half_rows):
            wait_z(layer, final, block, final + i)
            z = zbuf[layer, block, early:]
            zf = z.astype(F32)
            total = squares[block, :] + jnp.sum(zf * zf, axis=-1, keepdims=True)
            size = lax.rsqrt(total / width + 1e-06)
            product = jnp.dot(z, wout[layer, early:, :], preferred_element_type=F32)
            x = state[block, :] + size * (base[block, :] + product)
            state[block, :] = x
            if layer + 1 < LAYERS:
                normed[block, :] = normalise(x)
            else:
                pltpu.make_async_copy(state.at[block], out_hbm.at[block], out_sem.at[i]).start()
        if layer + 1 < LAYERS:
            queries(layer + 1)
            point("x")

    for i, block in enumerate(half_rows):
        pltpu.make_async_copy(state.at[block], out_hbm.at[block], out_sem.at[i]).wait()
    for copy in id_copies:
        copy.wait_send()
    for layer in range(LAYERS):
        wait(wout.at[layer, pl.ds(0, local)], wo_sem.at[2 + layer])

    def drain(u, _):
        layer, h = u // here, lax.rem(u, here)
        wait(kv.at[u, :, pl.ds(0, 2)], kv_send.at[u, 0])
        wait(kv.at[u, :, pl.ds(0, 2)], kv_send.at[u, 1])
        wait(kv.at[u, :, 2], kv_send.at[u, 2])
        wait(kv.at[u, :, 5], kv_send.at[u, 3])
        wait(kv.at[u, :, 0], kv_send.at[u, 4])
        wait(qown.at[layer, h], q_send.at[layer, h])
        return 0

    lax.fori_loop(0, units, drain, 0)
    for layer in range(LAYERS):
        for h in range(final):
            wait(psend.at[layer, h], p_send.at[layer, h])
            wait(psend.at[layer, h], z_send.at[layer, h])
        for i, block in enumerate(half_rows):
            wait(psend.at[layer, final, block], p_send.at[layer, final + i])
            wait(psend.at[layer, final, block], z_send.at[layer, final + i])


def on_device(ring, cand_embed, cand_ids, hist_ids, hist_len, hist_keys, hist_values, w_in, w_out):
    count, width = cand_embed.shape[1:]
    local = w_in.shape[3]
    head = width // HEADS
    here = local // head
    rows = hist_ids.shape[1]
    units = LAYERS * here
    dma = pltpu.SemaphoreType.DMA
    any_space = pl.BlockSpec(memory_space=pl.ANY)
    out = pl.pallas_call(
        functools.partial(kernel, (ring, rows, here, width, head)),
        out_shape=jax.ShapeDtypeStruct((count, width), F32),
        in_specs=[pl.BlockSpec(memory_space=pltpu.SMEM)] + [any_space] * 7,
        out_specs=any_space,
        scratch_shapes=[
            pltpu.VMEM((units, 2, 8, rows, head), BF),
            pltpu.VMEM((LAYERS, here, count, head), BF),
            pltpu.VMEM((LAYERS, here, count, head), BF),
            pltpu.VMEM((LAYERS, here, count, head), BF),
            pltpu.VMEM((LAYERS, here, count, head), BF),
            pltpu.VMEM((LAYERS, count, width), BF),
            pltpu.VMEM((here, count, head), BF),
            pltpu.VMEM((here, count, head), BF),
            pltpu.VMEM((here, count, head), F32),
            pltpu.VMEM((width, 4, local), BF),
            pltpu.VMEM((4, width, local), BF),
            pltpu.VMEM((LAYERS, width, width), BF),
            pltpu.VMEM((count, width), BF),
            pltpu.VMEM((count, width), F32),
            pltpu.VMEM((count, width), BF),
            pltpu.VMEM((3, 2, count, 8 * rows), BF),
            pltpu.VMEM((4, 1, count), jnp.int32),
            pltpu.VMEM((4 * ring, 1, rows), jnp.int32),
            pltpu.VMEM((here, count, head), F32),
            pltpu.VMEM((count, width), F32),
            pltpu.VMEM((count, 1), F32),
            dma((units, 8)),
            dma((units, 5)),
            dma((LAYERS, here)),
            dma((LAYERS, here)),
            dma((LAYERS, here + 1)),
            dma((LAYERS, here + 1)),
            dma((LAYERS, here + 1)),
            dma((LAYERS, here + 1)),
            dma((LAYERS,)),
            dma((2 * LAYERS,)),
            dma((LAYERS,)),
            dma((3,)),
            dma((4 * ring,)),
            dma((16,)),
            dma((3,)),
            dma((2,)),
        ],
        compiler_params=pltpu.CompilerParams(
            collective_id=0, has_side_effects=True, vmem_limit_bytes=60 * 1024 * 1024
        ),
        cost_estimate=pl.CostEstimate(
            flops=15 * 10**9, bytes_accessed=16 * 2**20, transcendentals=2 * 10**7
        ),
        name="hstu_layers",
    )(
        hist_len,
        cand_embed[0],
        cand_ids,
        hist_ids,
        hist_keys[0],
        hist_values[0],
        w_in,
        w_out,
    )
    return out[None]


def solution(mesh):
    in_specs = (
        P("user", "cand", None),
        P("user", "cand"),
        P("user", ("cand", "tensor")),
        P("user"),
        P("user", None, ("cand", "tensor"), None),
        P("user", None, ("cand", "tensor"), None),
        P(None, None, None, "tensor"),
        P(None, "tensor", None),
    )
    out_specs = P("user", "cand", None)
    ring = mesh.shape["cand"] // 2
    return jax.shard_map(
        functools.partial(on_device, ring),
        mesh=mesh,
        in_specs=in_specs,
        out_specs=out_specs,
        check_vma=False,
    )
```

```python
import functools

import jax
import jax.numpy as jnp
from jax import lax
from jax.experimental import pallas as pl
from jax.experimental.pallas import tpu as pltpu
from jax.sharding import PartitionSpec as P

HEADS = 8
LAYERS = 2
BF = jnp.bfloat16
KINDS = "RABRARBA"
OWN_FIRST = (0, 0)
ORDER = {
    "start": [(1, 0), (0, 0), (0, 1)],
    "o": [(1, 2), (1, 1), (0, 2)],
    "mask1": [(2, 0), (3, 0)],
    ("s", 0): [(1, 3), (2, 1), (3, 1), (0, 3)],
    ("n", 0): [(2, 2)],
    ("s", 1): [(3, 2)],
    ("n", 1): [(3, 3), (0, 4)],
    ("m", 2): [(2, 3)],
    ("s", 3): [(1, 5), (1, 4)],
    ("n", 3): [(0, 6)],
    "t": [(1, 6), (0, 5)],
    "w": [(2, 4), (3, 4)],
    "x": [(2, 5), (0, 7), (3, 5)],
    ("s", 4): [(1, 7)],
    ("m", 4): [(3, 6)],
    ("n", 4): [(2, 6)],
    ("m", 6): [(2, 7), (3, 7)],
}
F32 = jnp.float32


def gated(half):
    return half + half * jnp.tanh(half)


def kernel(
    dims,
    len_ref,
    embed_hbm,
    cid_hbm,
    hid_hbm,
    key_hbm,
    val_hbm,
    win_hbm,
    wout_hbm,
    out_hbm,
    kv,
    qown,
    qrem,
    psend,
    precv,
    zbuf,
    kown,
    vown,
    uown,
    raw,
    win,
    wout,
    embed,
    state,
    normed,
    mask,
    cids,
    hids,
    acc,
    base,
    squares,
    kv_recv,
    kv_send,
    q_recv,
    q_send,
    p_recv,
    p_send,
    z_recv,
    z_send,
    w_sem,
    wo_sem,
    wo_recv,
    cid_recv,
    hid_recv,
    id_send,
    loc_sem,
    out_sem,
):
    ring, rows, here, width, head = dims
    local = here * head
    count = state.shape[0]
    units = LAYERS * here
    scale = head ** (-0.5)

    cand = lax.axis_index("cand")
    t = lax.axis_index("tensor")
    y = lax.rem(cand, ring)
    plane = cand - y
    right = plane + lax.rem(y + 1, ring)
    left = plane + lax.rem(y + ring - 1, ring)
    far = plane + lax.rem(y + 2, ring)
    across = lax.rem(cand + ring, 2 * ring)
    near = y + 1 - 2 * lax.rem(y, 2)
    pairs = (plane + near, plane + ring - 1 - y)
    diagonals = (ring - plane + near, 2 * ring - 1 - plane - y)

    def roles(u):
        ringed = KINDS[u] == "R"
        pair, outer = pairs if KINDS[u] == "A" else pairs[::-1]
        diagonal = diagonals[0 if KINDS[u] == "A" else 1]
        return dict(
            first=pairs[0] if ringed else across,
            other=pairs[1] if ringed else pair,
            first_on=pairs[1] if ringed else pair,
            other_on=pairs[0] if ringed else across,
            partner=across if ringed else outer,
            origins=(cand, *pairs, far) if ringed else (cand, across, pair, diagonal),
            partner_ids={"R": 1, "A": 3, "B": 2}[KINDS[u]],
        )

    peers = [(cand, 1 - t)]
    for chip in (left, right, across, far, *diagonals):
        peers += [(chip, 0), (chip, 1)]

    embed_copy = pltpu.make_async_copy(embed_hbm, embed, loc_sem.at[0])
    embed_copy.start()

    def win_copy(layer):
        return pltpu.make_async_copy(win_hbm.at[layer], raw, w_sem.at[layer])

    win_copy(0).start()

    barrier = pltpu.get_barrier_semaphore()
    for chip, core in peers:
        pl.semaphore_signal(barrier, inc=1, device_id={"cand": chip, "tensor": core})
    pl.semaphore_wait(barrier, len(peers))

    def remote(src, dst, send, recv, chip, core):
        return pltpu.make_async_remote_copy(
            src_ref=src,
            dst_ref=dst,
            send_sem=send,
            recv_sem=recv,
            device_id={"cand": chip, "tensor": core},
        )

    def wait(ref, sem):
        pltpu.make_async_copy(ref, ref, sem).wait()

    row = cand * 2 + t
    hid_local = pltpu.make_async_copy(hid_hbm, hids.at[row], loc_sem.at[1])
    cid_local = pltpu.make_async_copy(cid_hbm, cids.at[0], loc_sem.at[2])
    id_copies = []
    for i, chip in enumerate((across, *pairs)):
        id_copies.append(
            remote(cid_hbm, cids.at[1 + i], id_send.at[i], cid_recv.at[i], chip, t)
        )
    for i, (chip, core) in enumerate(peers):
        id_copies.append(
            remote(hid_hbm, hids.at[row], id_send.at[3 + i], hid_recv.at[row], chip, core)
        )

    def on_chip(u, _):
        layer, h = u // here, lax.rem(u, here)
        own = pl.ds(pl.multiple_of(t * local + h * head, head), head)
        other = pl.ds(pl.multiple_of((1 - t) * local + h * head, head), head)
        for i, src in enumerate((key_hbm, val_hbm)):
            remote(
                src.at[layer, :, other],
                kv.at[u, i, t],
                kv_send.at[u, 4],
                kv_recv.at[u, t],
                cand,
                1 - t,
            ).start()
            pltpu.make_async_copy(
                src.at[layer, :, own], kv.at[u, i, t], kv_recv.at[u, t]
            ).start()
        return 0

    def direct(u, k):
        layer, h = u // here, u % here
        chip, slot = (roles(u)["first"], 2 + t) if k == 0 else (roles(u)["other"], 4 + t)
        for i, src in enumerate((key_hbm, val_hbm)):
            for core in (0, 1):
                cols = pl.ds(core * local + h * head, head)
                remote(
                    src.at[layer, :, cols],
                    kv.at[u, i, slot],
                    kv_send.at[u, k],
                    kv_recv.at[u, slot],
                    chip,
                    core,
                ).start()

    def forward(u, k):
        slot, to = ((2, 6), (5, 7))[k]
        chip = roles(u)[("first_on", "other_on")[k]]
        wait(kv.at[u, :, slot], kv_recv.at[u, slot])
        remote(
            kv.at[u, :, slot], kv.at[u, :, to], kv_send.at[u, 2 + k], kv_recv.at[u, to], chip, t
        ).start()

    def point(name):
        for step, u in ORDER.get(name, ()):
            (direct if step < 2 else forward)(u, step % 2)

    def unit_point(name, layer, h):
        for i in range(here - 1):
            if (name, layer * here + i) in ORDER:

                @pl.when(h == i)
                def _(i=i):
                    point((name, layer * here + i))

    point("start")
    hid_local.start()
    cid_local.start()
    for copy in id_copies:
        copy.start()

    def wout_copies(layer):
        copies = []
        for h in range(here):
            src = wout_hbm.at[layer, pl.ds(h * head, head)]
            dst = wout.at[layer, pl.ds(pl.multiple_of((h * 2 + t) * head, head), head)]
            copies += [
                pltpu.make_async_copy(src, dst, wo_sem.at[layer]),
                remote(src, dst, wo_sem.at[2 + layer], wo_recv.at[layer], cand, 1 - t),
            ]
        return copies

    def row_blocks(body, size):
        def step(i, _):
            body(pl.ds(pl.multiple_of(i * size, size), size))
            return 0

        lax.fori_loop(0, count // size, step, 0)

    def normalise(x):
        return (x * lax.rsqrt(jnp.mean(x * x, axis=-1, keepdims=True) + 1e-06)).astype(BF)

    embed_copy.wait()

    def first(block):
        x = embed[block, :].astype(F32)
        state[block, :] = x
        normed[block, :] = normalise(x)

    row_blocks(first, 128)

    def relay(layer):
        win_copy(layer).wait()

        def step(i, _):
            piece = pl.ds(pl.multiple_of(i * 64, 64), 64)
            win[:, piece, :] = jnp.swapaxes(raw[piece], 0, 1)
            return 0

        lax.fori_loop(0, width // 64, step, 0)

    def project(j):
        s = jnp.dot(normed[...], win[j], preferred_element_type=F32)
        return gated(0.5 * s)

    def split(ref, value):
        value = value.astype(ref.dtype)
        for h in range(here):
            ref[h] = value[:, h * head : (h + 1) * head]

    def queries(layer):
        split(qown.at[layer], project(2) * (0.5 * scale))
        for h in range(here):
            remote(
                qown.at[layer, h],
                qrem.at[layer, h],
                q_send.at[layer, h],
                q_recv.at[layer, h],
                roles(layer * here + h)["partner"],
                t,
            ).start()

    def others():
        for j, ref in ((3, kown), (1, vown), (0, uown)):
            split(ref, project(j))

    relay(0)
    win_copy(1).start()
    queries(0)
    point("q")
    others()
    point("o")
    lax.fori_loop(0, here, on_chip, 0)

    for copies in (wout_copies(0), wout_copies(1)):
        for copy in copies:
            copy.start()
    relay(1)

    hid_local.wait()
    cid_local.wait()
    for i in range(3):
        wait(cids.at[1 + i], cid_recv.at[i])
    for chip, core in peers:
        wait(hids.at[chip * 2 + core], hid_recv.at[chip * 2 + core])
    length = len_ref[0]

    def build_mask(kind):
        role = roles(KINDS.index("RAB"[kind]))
        for side in range(2):
            line = (role["partner_ids"], 0)[side]
            column = jnp.broadcast_to(cids[line].astype(F32), (128, count)).T
            for origin, chip in enumerate(role["origins"]):

                def one_core(core, _, side=side, column=column, origin=origin, chip=chip):
                    for part in range(rows // 128):
                        start = (chip * 2 + core) * rows + part * 128
                        at = start + lax.broadcasted_iota(jnp.int32, (1, 128), 1)
                        live = jnp.where(at < length, 1.0, 0.0).astype(F32)
                        piece = slice(part * 128, (part + 1) * 128)
                        ids = hids[chip * 2 + core, :, piece].astype(F32)
                        to = (origin * 2 + core) * rows + part * 128
                        to = pl.ds(pl.multiple_of(to, 128), 128)
                        mask[kind, side, :, to] = jnp.where(column == ids, 0.0, live).astype(BF)
                    return 0

                lax.fori_loop(0, 2, one_core, 0)

    for i, kind in enumerate(dict.fromkeys(KINDS)):
        build_mask("RAB".index(kind))
        point(f"mask{i}")
    lax.fori_loop(here, units, on_chip, 0)

    half_rows = [pl.ds(i * (count // 2), count // 2) for i in range(2)]
    all_rows = pl.ds(0, count)
    final = here - 1
    early = 2 * head * final

    def pick(values, h):
        result = jnp.int32(values[0])
        for i in range(1, len(values)):
            result = jnp.where(h == i, values[i], result)
        return result

    def attend(side, layer, h, u, kind, block):
        q = (qrem, qown)[side][layer, h, block, :]
        keys = kv[u, 0].reshape(8 * rows, head)
        values = kv[u, 1].reshape(8 * rows, head)
        half = lax.dot_general(
            q, keys, (((1,), (1,)), ((), ())), preferred_element_type=F32
        )
        weights = gated(half).astype(BF) * mask[kind, side, block, :]
        return jnp.dot(weights, values, preferred_element_type=F32)

    def send_part(layer, h, block, k):
        remote(
            psend.at[layer, h, block],
            precv.at[layer, h, block],
            p_send.at[layer, k],
            p_recv.at[layer, k],
            roles(layer * here + h)["partner"],
            t,
        ).start()

    def finish(layer, h, block, k):
        wait(precv.at[layer, h, block], p_recv.at[layer, k])
        q = qown[layer, h, block, :].astype(F32)
        own = gated(jnp.sum(q * kown[h, block, :].astype(F32), axis=-1, keepdims=True))
        total = acc[h, block, :] + precv[layer, h, block, :].astype(F32)
        total = (total + own * vown[h, block, :].astype(F32)) * uown[h, block, :]
        cols = pl.ds(pl.multiple_of((h * 2 + t) * head, head), head)
        zbuf[layer, block, cols] = total.astype(BF)
        remote(
            zbuf.at[layer, block, cols],
            zbuf.at[layer, block, cols],
            z_send.at[layer, k],
            z_recv.at[layer, k],
            cand,
            1 - t,
        ).start()

    def wait_z(layer, h, block, k):
        cols = pl.ds(pl.multiple_of((h * 2 + 1 - t) * head, head), head)
        wait(zbuf.at[layer, block, cols], z_recv.at[layer, k])

    def wait_kv(u):
        for slot in (0, 1, 3, 4, 6, 7):
            wait(kv.at[u, :, slot], kv_recv.at[u, slot])

    def drain(u, _):
        layer, h = u // here, lax.rem(u, here)
        wait(kv.at[u, :, pl.ds(0, 2)], kv_send.at[u, 0])
        wait(kv.at[u, :, pl.ds(0, 2)], kv_send.at[u, 1])
        wait(kv.at[u, :, 2], kv_send.at[u, 2])
        wait(kv.at[u, :, 5], kv_send.at[u, 3])
        wait(kv.at[u, :, 0], kv_send.at[u, 4])
        wait(qown.at[layer, h], q_send.at[layer, h])
        return 0

    for layer in range(LAYERS):
        kinds = ["RAB".index(kind) for kind in KINDS[layer * here : (layer + 1) * here]]

        def one_head(h, _, layer=layer, kinds=kinds):
            u = layer * here + h
            unit_point("s", layer, h)
            wait_kv(u)
            kind = pick(kinds[:final], h)
            for i in range(2):
                side = i ^ OWN_FIRST[layer]
                if side == 0:
                    wait(qrem.at[layer, h], q_recv.at[layer, h])
                if i == 0:
                    unit_point("m", layer, h)
                if side == 0:
                    psend[layer, h] = attend(0, layer, h, u, kind, all_rows).astype(BF)
                    for j in range(final):

                        @pl.when(h == j)
                        def _(j=j):
                            send_part(layer, j, all_rows, j)

                else:
                    acc[h] = attend(1, layer, h, u, kind, all_rows)
                if i == 0:
                    if layer > 0:
                        pl.when(h == 0)(others)
                    unit_point("n", layer, h)

            @pl.when(h > 0)
            def _():
                finish(layer, h - 1, all_rows, h - 1)

            return 0

        lax.fori_loop(0, final, one_head, 0)

        u = layer * here + final
        point(("s", u))
        wait_kv(u)
        wait(qrem.at[layer, final], q_recv.at[layer, final])
        point(("m", u))
        for i, block in enumerate(half_rows):
            psend[layer, final, block, :] = attend(0, layer, final, u, kinds[-1], block).astype(BF)
            send_part(layer, final, block, final + i)
        point(("n", u))
        finish(layer, final - 1, all_rows, final - 1)
        acc[final] = attend(1, layer, final, u, kinds[-1], all_rows)
        if layer == 0:
            point("t")
        else:
            lax.fori_loop(0, units - 2, drain, 0)
        wait(wout.at[layer, pl.ds(0, local)], wo_sem.at[layer])
        wait(wout.at[layer, pl.ds(0, local)], wo_recv.at[layer])
        for h in range(final):
            wait_z(layer, h, all_rows, h)
        z = zbuf[layer, :, :early]
        zf = z.astype(F32)
        squares[...] = jnp.sum(zf * zf, axis=-1, keepdims=True)
        base[...] = jnp.dot(z, wout[layer, :early, :], preferred_element_type=F32)
        for i, block in enumerate(half_rows):
            finish(layer, final, block, final + i)
        if layer == 0:
            point("w")
        for i, block in enumerate(half_rows):
            wait_z(layer, final, block, final + i)
            z = zbuf[layer, block, early:]
            zf = z.astype(F32)
            total = squares[block, :] + jnp.sum(zf * zf, axis=-1, keepdims=True)
            size = lax.rsqrt(total / width + 1e-06)
            product = jnp.dot(z, wout[layer, early:, :], preferred_element_type=F32)
            x = state[block, :] + size * (base[block, :] + product)
            state[block, :] = x
            if layer + 1 < LAYERS:
                normed[block, :] = normalise(x)
            else:
                pltpu.make_async_copy(state.at[block], out_hbm.at[block], out_sem.at[i]).start()
        if layer + 1 < LAYERS:
            queries(layer + 1)
            point("x")

    for i, block in enumerate(half_rows):
        pltpu.make_async_copy(state.at[block], out_hbm.at[block], out_sem.at[i]).wait()
    for copy in id_copies:
        copy.wait_send()
    for layer in range(LAYERS):
        wait(wout.at[layer, pl.ds(0, local)], wo_sem.at[2 + layer])

    lax.fori_loop(units - 2, units, drain, 0)
    for layer in range(LAYERS):
        for h in range(final):
            wait(psend.at[layer, h], p_send.at[layer, h])
            wait(psend.at[layer, h], z_send.at[layer, h])
        for i, block in enumerate(half_rows):
            wait(psend.at[layer, final, block], p_send.at[layer, final + i])
            wait(psend.at[layer, final, block], z_send.at[layer, final + i])


def on_device(ring, cand_embed, cand_ids, hist_ids, hist_len, hist_keys, hist_values, w_in, w_out):
    count, width = cand_embed.shape[1:]
    local = w_in.shape[3]
    head = width // HEADS
    here = local // head
    rows = hist_ids.shape[1]
    units = LAYERS * here
    dma = pltpu.SemaphoreType.DMA
    any_space = pl.BlockSpec(memory_space=pl.ANY)
    out = pl.pallas_call(
        functools.partial(kernel, (ring, rows, here, width, head)),
        out_shape=jax.ShapeDtypeStruct((count, width), F32),
        in_specs=[pl.BlockSpec(memory_space=pltpu.SMEM)] + [any_space] * 7,
        out_specs=any_space,
        scratch_shapes=[
            pltpu.VMEM((units, 2, 8, rows, head), BF),
            pltpu.VMEM((LAYERS, here, count, head), BF),
            pltpu.VMEM((LAYERS, here, count, head), BF),
            pltpu.VMEM((LAYERS, here, count, head), BF),
            pltpu.VMEM((LAYERS, here, count, head), BF),
            pltpu.VMEM((LAYERS, count, width), BF),
            pltpu.VMEM((here, count, head), BF),
            pltpu.VMEM((here, count, head), BF),
            pltpu.VMEM((here, count, head), F32),
            pltpu.VMEM((width, 4, local), BF),
            pltpu.VMEM((4, width, local), BF),
            pltpu.VMEM((LAYERS, width, width), BF),
            pltpu.VMEM((count, width), BF),
            pltpu.VMEM((count, width), F32),
            pltpu.VMEM((count, width), BF),
            pltpu.VMEM((3, 2, count, 8 * rows), BF),
            pltpu.VMEM((4, 1, count), jnp.int32),
            pltpu.VMEM((4 * ring, 1, rows), jnp.int32),
            pltpu.VMEM((here, count, head), F32),
            pltpu.VMEM((count, width), F32),
            pltpu.VMEM((count, 1), F32),
            dma((units, 8)),
            dma((units, 5)),
            dma((LAYERS, here)),
            dma((LAYERS, here)),
            dma((LAYERS, here + 1)),
            dma((LAYERS, here + 1)),
            dma((LAYERS, here + 1)),
            dma((LAYERS, here + 1)),
            dma((LAYERS,)),
            dma((2 * LAYERS,)),
            dma((LAYERS,)),
            dma((3,)),
            dma((4 * ring,)),
            dma((16,)),
            dma((3,)),
            dma((2,)),
        ],
        compiler_params=pltpu.CompilerParams(
            collective_id=0, has_side_effects=True, vmem_limit_bytes=60 * 1024 * 1024
        ),
        cost_estimate=pl.CostEstimate(
            flops=15 * 10**9, bytes_accessed=16 * 2**20, transcendentals=2 * 10**7
        ),
        name="hstu_layers",
    )(
        hist_len,
        cand_embed[0],
        cand_ids,
        hist_ids,
        hist_keys[0],
        hist_values[0],
        w_in,
        w_out,
    )
    return out[None]


def solution(mesh):
    in_specs = (
        P("user", "cand", None),
        P("user", "cand"),
        P("user", ("cand", "tensor")),
        P("user"),
        P("user", None, ("cand", "tensor"), None),
        P("user", None, ("cand", "tensor"), None),
        P(None, None, None, "tensor"),
        P(None, "tensor", None),
    )
    out_specs = P("user", "cand", None)
    ring = mesh.shape["cand"] // 2
    return jax.shard_map(
        functools.partial(on_device, ring),
        mesh=mesh,
        in_specs=in_specs,
        out_specs=out_specs,
        check_vma=False,
    )
```

```python
import functools

import jax
import jax.numpy as jnp
from jax import lax
from jax.experimental import pallas as pl
from jax.experimental.pallas import tpu as pltpu
from jax.sharding import PartitionSpec as P

HEADS = 8
LAYERS = 2
BF = jnp.bfloat16
KINDS = "RABRARBA"
OWN_FIRST = (0, 0)
ORDER = {
    "start": [(1, 0), (0, 0), (0, 1)],
    "o": [(1, 2), (1, 1), (0, 2)],
    "mask1": [(2, 0), (3, 0)],
    ("s", 0): [(1, 3), (2, 1), (3, 1), (0, 3)],
    ("n", 0): [(2, 2)],
    ("s", 1): [(3, 2)],
    ("n", 1): [(3, 3), (0, 4)],
    ("m", 2): [(2, 3)],
    ("s", 3): [(1, 5), (1, 4)],
    ("n", 3): [(0, 6)],
    "t": [(1, 6), (0, 5)],
    "w": [(2, 4), (3, 4)],
    "x": [(2, 5), (0, 7), (3, 5)],
    ("s", 4): [(1, 7)],
    ("m", 4): [(3, 6)],
    ("n", 4): [(2, 6)],
    ("m", 6): [(2, 7), (3, 7)],
}
F32 = jnp.float32


def gated(half):
    return half + half * jnp.tanh(half)


def kernel(
    dims,
    len_ref,
    embed_hbm,
    cid_hbm,
    hid_hbm,
    key_hbm,
    val_hbm,
    win_hbm,
    wout_hbm,
    out_hbm,
    kv,
    qown,
    qrem,
    psend,
    precv,
    zbuf,
    kown,
    vown,
    uown,
    raw,
    win,
    wout,
    embed,
    state,
    normed,
    mask,
    cids,
    hids,
    acc,
    base,
    squares,
    kv_recv,
    kv_send,
    q_recv,
    q_send,
    p_recv,
    p_send,
    z_recv,
    z_send,
    w_sem,
    wo_sem,
    wo_recv,
    cid_recv,
    hid_recv,
    id_send,
    loc_sem,
    out_sem,
):
    ring, rows, here, width, head = dims
    local = here * head
    count = state.shape[0]
    units = LAYERS * here
    scale = head ** (-0.5)

    cand = lax.axis_index("cand")
    t = lax.axis_index("tensor")
    y = lax.rem(cand, ring)
    plane = cand - y
    right = plane + lax.rem(y + 1, ring)
    left = plane + lax.rem(y + ring - 1, ring)
    far = plane + lax.rem(y + 2, ring)
    across = lax.rem(cand + ring, 2 * ring)
    near = y + 1 - 2 * lax.rem(y, 2)
    pairs = (plane + near, plane + ring - 1 - y)
    diagonals = (ring - plane + near, 2 * ring - 1 - plane - y)

    def roles(u):
        ringed = KINDS[u] == "R"
        pair, outer = pairs if KINDS[u] == "A" else pairs[::-1]
        diagonal = diagonals[0 if KINDS[u] == "A" else 1]
        return dict(
            first=pairs[0] if ringed else across,
            other=pairs[1] if ringed else pair,
            first_on=pairs[1] if ringed else pair,
            other_on=pairs[0] if ringed else across,
            partner=across if ringed else outer,
            origins=(cand, *pairs, far) if ringed else (cand, across, pair, diagonal),
            partner_ids={"R": 1, "A": 3, "B": 2}[KINDS[u]],
        )

    peers = [(cand, 1 - t)]
    for chip in (left, right, across, far, *diagonals):
        peers += [(chip, 0), (chip, 1)]

    embed_copy = pltpu.make_async_copy(embed_hbm, embed, loc_sem.at[0])
    embed_copy.start()

    def win_copy(layer):
        return pltpu.make_async_copy(win_hbm.at[layer], raw, w_sem.at[layer])

    win_copy(0).start()

    barrier = pltpu.get_barrier_semaphore()
    for chip, core in peers:
        pl.semaphore_signal(barrier, inc=1, device_id={"cand": chip, "tensor": core})
    pl.semaphore_wait(barrier, len(peers))

    def remote(src, dst, send, recv, chip, core):
        return pltpu.make_async_remote_copy(
            src_ref=src,
            dst_ref=dst,
            send_sem=send,
            recv_sem=recv,
            device_id={"cand": chip, "tensor": core},
        )

    def wait(ref, sem):
        pltpu.make_async_copy(ref, ref, sem).wait()

    row = cand * 2 + t
    hid_local = pltpu.make_async_copy(hid_hbm, hids.at[row], loc_sem.at[1])
    cid_local = pltpu.make_async_copy(cid_hbm, cids.at[0], loc_sem.at[2])
    id_copies = []
    for i, chip in enumerate((across, *pairs)):
        id_copies.append(
            remote(cid_hbm, cids.at[1 + i], id_send.at[i], cid_recv.at[i], chip, t)
        )
    for i, (chip, core) in enumerate(peers):
        id_copies.append(
            remote(hid_hbm, hids.at[row], id_send.at[3 + i], hid_recv.at[row], chip, core)
        )

    def on_chip(u, _):
        layer, h = u // here, lax.rem(u, here)
        own = pl.ds(pl.multiple_of(t * local + h * head, head), head)
        other = pl.ds(pl.multiple_of((1 - t) * local + h * head, head), head)
        for i, src in enumerate((key_hbm, val_hbm)):
            remote(
                src.at[layer, :, other],
                kv.at[u, i, t],
                kv_send.at[u, 4],
                kv_recv.at[u, t],
                cand,
                1 - t,
            ).start()
            pltpu.make_async_copy(
                src.at[layer, :, own], kv.at[u, i, t], kv_recv.at[u, t]
            ).start()
        return 0

    def direct(u, k):
        layer, h = u // here, u % here
        chip, slot = (roles(u)["first"], 2 + t) if k == 0 else (roles(u)["other"], 4 + t)
        for i, src in enumerate((key_hbm, val_hbm)):
            for core in (0, 1):
                cols = pl.ds(core * local + h * head, head)
                remote(
                    src.at[layer, :, cols],
                    kv.at[u, i, slot],
                    kv_send.at[u, k],
                    kv_recv.at[u, slot],
                    chip,
                    core,
                ).start()

    def forward(u, k):
        slot, to = ((2, 6), (5, 7))[k]
        chip = roles(u)[("first_on", "other_on")[k]]
        wait(kv.at[u, :, slot], kv_recv.at[u, slot])
        remote(
            kv.at[u, :, slot], kv.at[u, :, to], kv_send.at[u, 2 + k], kv_recv.at[u, to], chip, t
        ).start()

    def point(name):
        for step, u in ORDER.get(name, ()):
            (direct if step < 2 else forward)(u, step % 2)

    def unit_point(name, layer, h):
        for i in range(here - 1):
            if (name, layer * here + i) in ORDER:

                @pl.when(h == i)
                def _(i=i):
                    point((name, layer * here + i))

    point("start")
    hid_local.start()
    cid_local.start()
    for copy in id_copies:
        copy.start()

    def wout_copies(layer):
        copies = []
        for h in range(here):
            src = wout_hbm.at[layer, pl.ds(h * head, head)]
            dst = wout.at[layer, pl.ds(pl.multiple_of((h * 2 + t) * head, head), head)]
            copies += [
                pltpu.make_async_copy(src, dst, wo_sem.at[layer]),
                remote(src, dst, wo_sem.at[2 + layer], wo_recv.at[layer], cand, 1 - t),
            ]
        return copies

    def row_blocks(body, size):
        def step(i, _):
            body(pl.ds(pl.multiple_of(i * size, size), size))
            return 0

        lax.fori_loop(0, count // size, step, 0)

    def normalise(x):
        return (x * lax.rsqrt(jnp.mean(x * x, axis=-1, keepdims=True) + 1e-06)).astype(BF)

    embed_copy.wait()

    def first(block):
        x = embed[block, :].astype(F32)
        state[block, :] = x
        normed[block, :] = normalise(x)

    row_blocks(first, 128)

    def relay(layer):
        win_copy(layer).wait()

        def step(i, _):
            piece = pl.ds(pl.multiple_of(i * 64, 64), 64)
            win[:, piece, :] = jnp.swapaxes(raw[piece], 0, 1)
            return 0

        lax.fori_loop(0, width // 64, step, 0)

    def project(j):
        s = jnp.dot(normed[...], win[j], preferred_element_type=F32)
        return gated(0.5 * s)

    def split(ref, value):
        value = value.astype(ref.dtype)
        for h in range(here):
            ref[h] = value[:, h * head : (h + 1) * head]

    def queries(layer):
        split(qown.at[layer], project(2) * (0.5 * scale))
        for h in range(here):
            remote(
                qown.at[layer, h],
                qrem.at[layer, h],
                q_send.at[layer, h],
                q_recv.at[layer, h],
                roles(layer * here + h)["partner"],
                t,
            ).start()

    def others():
        for j, ref in ((3, kown), (1, vown), (0, uown)):
            split(ref, project(j))

    relay(0)
    win_copy(1).start()
    queries(0)
    point("q")
    others()
    point("o")
    lax.fori_loop(0, here, on_chip, 0)

    for copies in (wout_copies(0), wout_copies(1)):
        for copy in copies:
            copy.start()
    relay(1)

    hid_local.wait()
    cid_local.wait()
    for i in range(3):
        wait(cids.at[1 + i], cid_recv.at[i])
    for chip, core in peers:
        wait(hids.at[chip * 2 + core], hid_recv.at[chip * 2 + core])
    length = len_ref[0]

    def build_mask(kind):
        role = roles(KINDS.index("RAB"[kind]))
        for side in range(2):
            line = (role["partner_ids"], 0)[side]
            column = jnp.broadcast_to(cids[line].astype(F32), (128, count)).T
            for origin, chip in enumerate(role["origins"]):

                def one_core(core, _, side=side, column=column, origin=origin, chip=chip):
                    for part in range(rows // 128):
                        start = (chip * 2 + core) * rows + part * 128
                        at = start + lax.broadcasted_iota(jnp.int32, (1, 128), 1)
                        live = jnp.where(at < length, 1.0, 0.0).astype(F32)
                        piece = slice(part * 128, (part + 1) * 128)
                        ids = hids[chip * 2 + core, :, piece].astype(F32)
                        to = (origin * 2 + core) * rows + part * 128
                        to = pl.ds(pl.multiple_of(to, 128), 128)
                        mask[kind, side, :, to] = jnp.where(column == ids, 0.0, live).astype(BF)
                    return 0

                lax.fori_loop(0, 2, one_core, 0)

    for i, kind in enumerate(dict.fromkeys(KINDS)):
        build_mask("RAB".index(kind))
        point(f"mask{i}")
    lax.fori_loop(here, units, on_chip, 0)

    half_rows = [pl.ds(i * (count // 2), count // 2) for i in range(2)]
    all_rows = pl.ds(0, count)
    final = here - 1
    early = 2 * head * final

    def pick(values, h):
        result = jnp.int32(values[0])
        for i in range(1, len(values)):
            result = jnp.where(h == i, values[i], result)
        return result

    def attend(side, layer, h, u, kind, block):
        q = (qrem, qown)[side][layer, h, block, :]
        keys = kv[u, 0].reshape(8 * rows, head)
        values = kv[u, 1].reshape(8 * rows, head)
        half = lax.dot_general(
            q, keys, (((1,), (1,)), ((), ())), preferred_element_type=F32
        )
        weights = gated(half).astype(BF) * mask[kind, side, block, :]
        return jnp.dot(weights, values, preferred_element_type=F32)

    def send_part(layer, h, block, k):
        remote(
            psend.at[layer, h, block],
            precv.at[layer, h, block],
            p_send.at[layer, k],
            p_recv.at[layer, k],
            roles(layer * here + h)["partner"],
            t,
        ).start()

    def finish(layer, h, block, k):
        wait(precv.at[layer, h, block], p_recv.at[layer, k])
        q = qown[layer, h, block, :].astype(F32)
        own = gated(jnp.sum(q * kown[h, block, :].astype(F32), axis=-1, keepdims=True))
        total = acc[h, block, :] + precv[layer, h, block, :].astype(F32)
        total = (total + own * vown[h, block, :].astype(F32)) * uown[h, block, :]
        cols = pl.ds(pl.multiple_of((h * 2 + t) * head, head), head)
        zbuf[layer, block, cols] = total.astype(BF)
        remote(
            zbuf.at[layer, block, cols],
            zbuf.at[layer, block, cols],
            z_send.at[layer, k],
            z_recv.at[layer, k],
            cand,
            1 - t,
        ).start()

    def wait_z(layer, h, block, k):
        cols = pl.ds(pl.multiple_of((h * 2 + 1 - t) * head, head), head)
        wait(zbuf.at[layer, block, cols], z_recv.at[layer, k])

    def wait_kv(u):
        for slot in (0, 1, 3, 4, 6, 7):
            wait(kv.at[u, :, slot], kv_recv.at[u, slot])

    def drain(u, _):
        layer, h = u // here, lax.rem(u, here)
        wait(kv.at[u, :, pl.ds(0, 2)], kv_send.at[u, 0])
        wait(kv.at[u, :, pl.ds(0, 2)], kv_send.at[u, 1])
        wait(kv.at[u, :, 2], kv_send.at[u, 2])
        wait(kv.at[u, :, 5], kv_send.at[u, 3])
        wait(kv.at[u, :, 0], kv_send.at[u, 4])
        wait(qown.at[layer, h], q_send.at[layer, h])
        return 0

    for layer in range(LAYERS):
        kinds = ["RAB".index(kind) for kind in KINDS[layer * here : (layer + 1) * here]]

        def one_head(h, _, layer=layer, kinds=kinds):
            u = layer * here + h
            unit_point("s", layer, h)
            wait_kv(u)
            kind = pick(kinds[:final], h)
            for i in range(2):
                side = i ^ OWN_FIRST[layer]
                if side == 0:
                    wait(qrem.at[layer, h], q_recv.at[layer, h])
                if i == 0:
                    unit_point("m", layer, h)
                if side == 0:
                    psend[layer, h] = attend(0, layer, h, u, kind, all_rows).astype(BF)
                    for j in range(final):

                        @pl.when(h == j)
                        def _(j=j):
                            send_part(layer, j, all_rows, j)

                else:
                    acc[h] = attend(1, layer, h, u, kind, all_rows)
                if i == 0:
                    if layer > 0:
                        pl.when(h == 0)(others)
                    unit_point("n", layer, h)

            @pl.when(h > 0)
            def _():
                finish(layer, h - 1, all_rows, h - 1)

            return 0

        lax.fori_loop(0, final, one_head, 0)

        u = layer * here + final
        point(("s", u))
        wait_kv(u)
        wait(qrem.at[layer, final], q_recv.at[layer, final])
        point(("m", u))
        for i, block in enumerate(half_rows):
            psend[layer, final, block, :] = attend(0, layer, final, u, kinds[-1], block).astype(BF)
            send_part(layer, final, block, final + i)
        point(("n", u))
        finish(layer, final - 1, all_rows, final - 1)
        acc[final] = attend(1, layer, final, u, kinds[-1], all_rows)
        if layer == 0:
            point("t")
        else:
            lax.fori_loop(0, units - 2, drain, 0)
        wait(wout.at[layer, pl.ds(0, local)], wo_sem.at[layer])
        wait(wout.at[layer, pl.ds(0, local)], wo_recv.at[layer])
        for h in range(final):
            wait_z(layer, h, all_rows, h)
        z = zbuf[layer, :, :early]
        zf = z.astype(F32)
        squares[...] = jnp.sum(zf * zf, axis=-1, keepdims=True)
        base[...] = jnp.dot(z, wout[layer, :early, :], preferred_element_type=F32)
        for i, block in enumerate(half_rows):
            finish(layer, final, block, final + i)
        if layer == 0:
            point("w")
        for i, block in enumerate(half_rows):
            wait_z(layer, final, block, final + i)
            z = zbuf[layer, block, early:]
            zf = z.astype(F32)
            total = squares[block, :] + jnp.sum(zf * zf, axis=-1, keepdims=True)
            size = lax.rsqrt(total / width + 1e-06)
            product = jnp.dot(z, wout[layer, early:, :], preferred_element_type=F32)
            x = state[block, :] + size * (base[block, :] + product)
            state[block, :] = x
            if layer + 1 < LAYERS:
                normed[block, :] = normalise(x)
            else:
                pltpu.make_async_copy(state.at[block], out_hbm.at[block], out_sem.at[i]).start()
        if layer + 1 < LAYERS:
            queries(layer + 1)
            point("x")

    for i, block in enumerate(half_rows):
        pltpu.make_async_copy(state.at[block], out_hbm.at[block], out_sem.at[i]).wait()
    for copy in id_copies:
        copy.wait_send()
    for layer in range(LAYERS):
        wait(wout.at[layer, pl.ds(0, local)], wo_sem.at[2 + layer])

    lax.fori_loop(units - 2, units, drain, 0)
    for layer in range(LAYERS):
        for h in range(final):
            wait(psend.at[layer, h], p_send.at[layer, h])
            wait(psend.at[layer, h], z_send.at[layer, h])
        for i, block in enumerate(half_rows):
            wait(psend.at[layer, final, block], p_send.at[layer, final + i])
            wait(psend.at[layer, final, block], z_send.at[layer, final + i])


def pass_on(x_hbm, out_hbm, x, in_sem, out_sem):
    size = x.shape[0] // in_sem.shape[0]
    blocks = [pl.ds(i * size, size) for i in range(in_sem.shape[0])]
    ins = [
        pltpu.make_async_copy(x_hbm.at[block], x.at[block], in_sem.at[i])
        for i, block in enumerate(blocks)
    ]
    outs = [
        pltpu.make_async_copy(x.at[block], out_hbm.at[block], out_sem.at[i])
        for i, block in enumerate(blocks)
    ]
    for copy in ins:
        copy.start()
    for arrived, leaving in zip(ins, outs):
        arrived.wait()
        leaving.start()
    for copy in outs:
        copy.wait()


def on_device(ring, cand_embed, cand_ids, hist_ids, hist_len, hist_keys, hist_values, w_in, w_out):
    count, width = cand_embed.shape[1:]
    local = w_in.shape[3]
    head = width // HEADS
    here = local // head
    rows = hist_ids.shape[1]
    units = LAYERS * here
    dma = pltpu.SemaphoreType.DMA
    any_space = pl.BlockSpec(memory_space=pl.ANY)
    out = pl.pallas_call(
        functools.partial(kernel, (ring, rows, here, width, head)),
        out_shape=jax.ShapeDtypeStruct((count, width), F32),
        in_specs=[pl.BlockSpec(memory_space=pltpu.SMEM)] + [any_space] * 7,
        out_specs=any_space,
        scratch_shapes=[
            pltpu.VMEM((units, 2, 8, rows, head), BF),
            pltpu.VMEM((LAYERS, here, count, head), BF),
            pltpu.VMEM((LAYERS, here, count, head), BF),
            pltpu.VMEM((LAYERS, here, count, head), BF),
            pltpu.VMEM((LAYERS, here, count, head), BF),
            pltpu.VMEM((LAYERS, count, width), BF),
            pltpu.VMEM((here, count, head), BF),
            pltpu.VMEM((here, count, head), BF),
            pltpu.VMEM((here, count, head), F32),
            pltpu.VMEM((width, 4, local), BF),
            pltpu.VMEM((4, width, local), BF),
            pltpu.VMEM((LAYERS, width, width), BF),
            pltpu.VMEM((count, width), BF),
            pltpu.VMEM((count, width), F32),
            pltpu.VMEM((count, width), BF),
            pltpu.VMEM((3, 2, count, 8 * rows), BF),
            pltpu.VMEM((4, 1, count), jnp.int32),
            pltpu.VMEM((4 * ring, 1, rows), jnp.int32),
            pltpu.VMEM((here, count, head), F32),
            pltpu.VMEM((count, width), F32),
            pltpu.VMEM((count, 1), F32),
            dma((units, 8)),
            dma((units, 5)),
            dma((LAYERS, here)),
            dma((LAYERS, here)),
            dma((LAYERS, here + 1)),
            dma((LAYERS, here + 1)),
            dma((LAYERS, here + 1)),
            dma((LAYERS, here + 1)),
            dma((LAYERS,)),
            dma((2 * LAYERS,)),
            dma((LAYERS,)),
            dma((3,)),
            dma((4 * ring,)),
            dma((16,)),
            dma((3,)),
            dma((2,)),
        ],
        compiler_params=pltpu.CompilerParams(
            collective_id=0, has_side_effects=True, vmem_limit_bytes=60 * 1024 * 1024
        ),
        cost_estimate=pl.CostEstimate(
            flops=15 * 10**9, bytes_accessed=16 * 2**20, transcendentals=2 * 10**7
        ),
        name="hstu_layers",
    )(
        hist_len,
        cand_embed[0],
        cand_ids,
        hist_ids,
        hist_keys[0],
        hist_values[0],
        w_in,
        w_out,
    )
    return pl.pallas_call(
        pass_on,
        out_shape=jax.ShapeDtypeStruct((count, width), F32),
        in_specs=[any_space],
        out_specs=any_space,
        scratch_shapes=[pltpu.VMEM((count, width), F32), dma((8,)), dma((8,))],
        compiler_params=pltpu.CompilerParams(vmem_limit_bytes=60 * 1024 * 1024),
        name="pass_on",
    )(out)[None]


def solution(mesh):
    in_specs = (
        P("user", "cand", None),
        P("user", "cand"),
        P("user", ("cand", "tensor")),
        P("user"),
        P("user", None, ("cand", "tensor"), None),
        P("user", None, ("cand", "tensor"), None),
        P(None, None, None, "tensor"),
        P(None, "tensor", None),
    )
    out_specs = P("user", "cand", None)
    ring = mesh.shape["cand"] // 2
    return jax.shard_map(
        functools.partial(on_device, ring),
        mesh=mesh,
        in_specs=in_specs,
        out_specs=out_specs,
        check_vma=False,
    )
```
